512 devices in a mesh: sec: 4 (over z_hi, core), gx: 32 (over y, z_lo), gy: 4 (over x).
Axes of the slice: x: 4, y: 4, z: 16 (z_hi: 2, z_lo: 8; z = z_hi * 8 + z_lo), core: 2. Of those that a mesh axis runs over, the one named last changes fastest.
Arguments:
- adjoint: float32 [4, 5, 256, 32, 128], P('sec', None, 'gx', 'gy'), may hold values from -6 to 6
- flow: float32 [4, 6, 256, 32, 128], P('sec', None, 'gx', 'gy'), as said below
- point_cell: int32 [4, 32, 4, 1024], P('sec', 'gx', 'gy'), may hold values from 0 to 8191
- point_dest: int32 [4, 32, 4, 1024], P('sec', 'gx', 'gy'), may hold values from 0 to 127, as said below
- point_target: int32 [4, 32, 4, 1024], P('sec', 'gx', 'gy'), may hold values from 0 to 8191
- point_weight: float32 [4, 32, 4, 1024], P('sec', 'gx', 'gy'), may hold values from 0.5 to 2
- point_count: int32 [4, 32, 4], P('sec', 'gx', 'gy'), may hold values from 0 to 1024, as said below
Outputs:
- adjoint_next: float32 [4, 5, 256, 32, 128], P('sec', None, 'gx', 'gy')
The draws below stay inside these ranges and needn't reach their ends.
Inputs may be any that keep to these rules, and one draw needn't show every extreme that they name: `flow`: density 0.6 to 1.6, pressure 0.4 (E - kinetic) from 0.5 to 1.5, sponge rate 0.05 to 1. `point_count`: zero on the near-field section; on far-field tiles a multiple of 128, reaching 1024 on some tile. `point_dest`: among the live slots of one far-field tile at most 20 name the same near-field tile, and 20 is reached. Near-field tiles receive unequal numbers of points.
All inputs are finite; a program needn't handle non-finite values.
Results may differ from the reference program's by a relative error of at most 0.00002.
Values sent between devices are 32-bit elements; how exact they have to be, the bound alone decides.
A program may use at most 64 MiB of HBM per device.

```python
import math
import jax
import jax.numpy as jnp
from jax import lax

CX = 8
CY = 8
CZ = 128
PTS_DEV = 1024
ADJ_FIELDS = 5
SECTIONS = 4
NX = 256
NY = 32
NZ = 128
NTILE = 128
N_GX = 32
N_GY = 4


def draw_flow(key, part):
    keys = jax.random.split(key, 4)
    grid_shape = (SECTIONS, NX, NY, NZ)
    density = jax.random.uniform(keys[0], grid_shape, jnp.float32, 0.6, 1.6)
    velocity = 0.4 * jax.random.normal(keys[1], (3,) + grid_shape, jnp.float32)
    pressure = jax.random.uniform(keys[2], grid_shape, jnp.float32, 0.5, 1.5)
    sponge = jnp.exp(jax.random.uniform(keys[3], grid_shape, jnp.float32, math.log(0.05), 0.0))
    momenta = density[None] * velocity
    energy = pressure / 0.4 + 0.5 * density * jnp.sum(velocity * velocity, axis=0)
    return jnp.stack([density, momenta[0], momenta[1], momenta[2], energy, sponge], axis=1).astype(jnp.float32)


def draw_point_count(key, part):
    first_key, second_key = jax.random.split(key)
    tiles_x = NX // CX
    tiles_y = NY // CY
    base_count = 128 * jax.random.randint(first_key, (SECTIONS, tiles_x, tiles_y), PTS_DEV // 256, PTS_DEV // 128 + 1)
    chosen = jax.random.randint(second_key, (), 0, (SECTIONS - 1) * NTILE)
    flat_index = jnp.arange(SECTIONS * NTILE, dtype=jnp.int32).reshape(SECTIONS, tiles_x, tiles_y)
    base_count = jnp.where(flat_index == chosen, PTS_DEV, base_count)
    section_index = jnp.arange(SECTIONS, dtype=jnp.int32)[:, None, None]
    return jnp.where(section_index == SECTIONS - 1, 0, base_count).astype(jnp.int32)


def draw_point_dest(key, part):
    first_key, second_key = jax.random.split(key)
    shuffle = jax.random.permutation(first_key, NTILE)
    tile_keys = jax.random.split(second_key, SECTIONS * NTILE)
    slot_order = jax.vmap(lambda one_key: jax.random.permutation(one_key, PTS_DEV))(tile_keys)
    half_slots = PTS_DEV // 2
    hashed = jnp.where(slot_order < half_slots, slot_order % NTILE, (slot_order - half_slots) % (NTILE // 4))
    return shuffle[hashed].reshape(SECTIONS, NX // CX, NY // CY, PTS_DEV).astype(jnp.int32)


def with_ends(result, rng, least, largest):
    spot = [jax.random.randint(jax.random.fold_in(rng, axis), (), 0, length) for axis, length in enumerate(result.shape)]
    longest = result.shape.index(max(result.shape))
    neighbour = spot[:longest] + [(spot[longest] + 1) % result.shape[longest]] + spot[longest + 1:]
    return result.at[tuple(spot)].set(least).at[tuple(neighbour)].set(largest)


def block_levels(rng, shape, pieces, least, high):
    loudness, own = 1.0, jax.random.fold_in(rng, 6)
    for axis_at, blocks in pieces:
        draws = jnp.exp(jax.random.uniform(jax.random.fold_in(own, axis_at), (blocks,), jnp.float32, least / len(pieces), high / len(pieces)))
        loudness = loudness * jnp.repeat(draws, shape[axis_at] // blocks).reshape([-1 if axis == axis_at else 1 for axis in range(len(shape))])
    return loudness


def noise(own_key, dims, spread, most, shards=(), kind=jnp.bfloat16):
    values = jax.random.normal(own_key, dims, jnp.float32) * spread
    if len(shards) > 0:
        values = block_levels(own_key, dims, shards, -0.22, 0.18) * values
    return jnp.clip(values, min=-most, max=most).astype(kind)


def setup_inputs(seed: int = 0) -> dict:
    key_list = jax.random.split(jax.random.key(seed), 8)
    adjoint = noise(key_list[0], (SECTIONS, ADJ_FIELDS, NX, NY, NZ), 1.0, 6.0, ((0, 4), (2, 32), (3, 4)), jnp.float32)
    flow = draw_flow(jax.random.fold_in(key_list[7], 71), 0)
    point_cell = with_ends(jax.random.randint(key_list[2], (SECTIONS, N_GX, N_GY, PTS_DEV), 0, CX * CY * CZ), jax.random.fold_in(key_list[2], 1), 0, (CX * CY * CZ) - 1).astype(jnp.int32)
    point_dest = draw_point_dest(jax.random.fold_in(key_list[7], 71), 0)
    point_target = with_ends(jax.random.randint(key_list[4], (SECTIONS, N_GX, N_GY, PTS_DEV), 0, CX * CY * CZ), jax.random.fold_in(key_list[4], 1), 0, (CX * CY * CZ) - 1).astype(jnp.int32)
    point_weight = jnp.clip(jnp.exp(math.log(2.0) - 1.3862944 * jax.random.uniform(key_list[5], (SECTIONS, N_GX, N_GY, PTS_DEV), jnp.float32) ** block_levels(key_list[5], (SECTIONS, N_GX, N_GY, PTS_DEV), ((0, 4), (1, 32), (2, 4)), -0.2, 0.2)), 0.5, 2.0)
    point_count = draw_point_count(jax.random.fold_in(key_list[7], 71), 0)
    return {"adjoint": adjoint, "flow": flow, "point_cell": point_cell, "point_dest": point_dest, "point_target": point_target, "point_weight": point_weight, "point_count": point_count}


GAMMA_MINUS = 0.4
GAMMA_RATIO = 1.4
STEP_SIZE = 0.4


def shifted(padded, offset, along):
    length = padded.shape[along] - 6
    return lax.slice_in_dim(padded, 3 + offset, 3 + offset + length, axis=along)


def stencil(padded, along):
    first = shifted(padded, 1, along) - shifted(padded, -1, along)
    second = shifted(padded, 2, along) - shifted(padded, -2, along)
    third = shifted(padded, 3, along) - shifted(padded, -3, along)
    return (45.0 * first - 9.0 * second + third) / 60.0


def wrap_last(values_in):
    return jnp.concatenate([values_in[..., -3:], values_in, values_in[..., :3]], axis=-1)


def fluxes(adjoint, flow, direction):
    density = flow[0]
    inverse = 1.0 / density
    momenta = flow[1:4]
    velocity = momenta[direction] * inverse
    kinetic = 0.5 * (momenta[0] * momenta[0] + momenta[1] * momenta[1] + momenta[2] * momenta[2]) * inverse
    pressure = GAMMA_MINUS * (flow[4] - kinetic)
    stiffness = GAMMA_RATIO * pressure
    return jnp.stack([velocity * adjoint[0], velocity * adjoint[1], velocity * adjoint[2],
                      velocity * adjoint[3], velocity * adjoint[4],
                      density * adjoint[0] + stiffness * adjoint[4],
                      adjoint[1 + direction] * inverse])


def assemble(adjoint, flow, along_x, along_y, along_z, source):
    summed = along_x + along_y + along_z
    rate_list = jnp.stack([summed[0], summed[1] + along_x[5], summed[2] + along_y[5],
                           summed[3] + along_z[5], summed[4] + summed[6]])
    return adjoint + STEP_SIZE * (rate_list - flow[5] * adjoint + source)


def section_segment(adjoint, flow, source):
    flux_x = fluxes(adjoint, flow, 0)
    along_x = stencil(jnp.pad(flux_x, ((0, 0), (3, 3), (0, 0), (0, 0))), 1)
    flux_y = fluxes(adjoint, flow, 1)
    along_y = stencil(jnp.pad(flux_y, ((0, 0), (0, 0), (3, 3), (0, 0))), 2)
    along_z = stencil(wrap_last(fluxes(adjoint, flow, 2)), 3)
    return assemble(adjoint, flow, along_x, along_y, along_z, source)


def gather_sources(adjoint, point_cell, point_dest, point_target, point_weight, point_count):
    cell_count = CX * CY * CZ
    blocks = adjoint.reshape(SECTIONS, ADJ_FIELDS, N_GX, CX, N_GY, CY, CZ)
    blocks = blocks.transpose(0, 2, 4, 1, 3, 5, 6).reshape(SECTIONS, NTILE, ADJ_FIELDS, cell_count)
    pick_index = jnp.broadcast_to(point_cell.reshape(SECTIONS, NTILE, 1, PTS_DEV), (SECTIONS, NTILE, ADJ_FIELDS, PTS_DEV))
    values = jnp.take_along_axis(blocks, pick_index, axis=3)
    live_mask = jnp.arange(PTS_DEV, dtype=jnp.int32)[None, None, :] < point_count.reshape(SECTIONS, NTILE, 1)
    scaled = values * point_weight.reshape(SECTIONS, NTILE, 1, PTS_DEV) * live_mask[:, :, None, :].astype(values.dtype)
    flat_values = scaled.transpose(0, 1, 3, 2).reshape(-1, ADJ_FIELDS)
    dest_flat = point_dest.reshape(-1)
    targets = point_target.reshape(-1)
    gathered = jnp.zeros((NTILE, ADJ_FIELDS, cell_count), jnp.float32).at[dest_flat, :, targets].add(flat_values)
    gathered = gathered.reshape(N_GX, N_GY, ADJ_FIELDS, CX, CY, CZ).transpose(2, 0, 3, 1, 4, 5)
    return gathered.reshape(ADJ_FIELDS, NX, NY, NZ)


def reference(adjoint, flow, point_cell, point_dest, point_target, point_weight, point_count):
    near_source = gather_sources(adjoint, point_cell, point_dest, point_target, point_weight, point_count)
    outputs = []
    for section in range(SECTIONS):
        if section == SECTIONS - 1:
            source = near_source
        else:
            source = jnp.zeros_like(near_source)
        outputs.append(section_segment(adjoint[section], flow[section], source))
    return jnp.stack(outputs)
```

```python
import jax
import jax.numpy as jnp
from jax import lax
from jax.experimental import pallas as pl
from jax.experimental.pallas import tpu as pltpu
from jax.sharding import PartitionSpec as P

GAMMA_MINUS = 0.4
GAMMA_RATIO = 1.4
STEP_SIZE = 0.4
FAR = 3
NZ_DEV = 8
NY_DEV = 4
NX_DEV = 4
PLANE = NY_DEV * NX_DEV
SLOTS = 20
F32 = jnp.float32
BF16 = jnp.bfloat16


def iota(shape, dim):
    return lax.broadcasted_iota(jnp.int32, shape, dim)


def two_parts(x):
    high = x.astype(BF16).astype(F32)
    return high, (x - high).astype(BF16).astype(F32)


def onehot(condition):
    return jnp.where(condition, 1.0, 0.0).astype(BF16)


def word_row(word, slot):
    base = 40 * (word // 2)
    return base + slot if word % 2 == 0 else base + 20 + (slot + 4) % 20


def pack(adjoint, cell, dest, target, weight, count):
    points = cell.shape[1]
    live = iota((1, points), 1) < count
    row, lane = cell >> 7, cell & 127
    lanes = onehot(iota((128, points), 0) == lane)
    high, low = two_parts(adjoint)
    parts = jnp.concatenate([high.astype(BF16), low.astype(BF16)], axis=1)
    picked = jnp.dot(
        parts, jnp.concatenate([lanes, lanes], axis=0), preferred_element_type=F32
    )
    row_mask = iota((64, points), 0) == row
    scale = jnp.where(live, weight, 0.0)
    words = [
        jnp.sum(
            jnp.where(row_mask, picked[64 * f : 64 * f + 64], 0.0),
            axis=0,
            keepdims=True,
        )
        * scale
        for f in range(5)
    ]
    words.append(target.astype(F32))
    place = (dest & 96) | ((dest & 3) << 3) | ((dest >> 2) & 7)
    place = jnp.where(live, place, -1)
    tiles = jnp.where(iota((128, points), 0) == place, 1.0, 0.0)
    tiles16 = tiles.astype(BF16)
    before = onehot(iota((256, 256), 0) < iota((256, 256), 1))
    ranks = []
    earlier = jnp.zeros((128, 1), F32)
    for b in range(points // 256):
        block = tiles[:, 256 * b : 256 * b + 256]
        counts = jnp.dot(
            tiles16[:, 256 * b : 256 * b + 256], before, preferred_element_type=F32
        )
        ranks.append(jnp.sum(block * (counts + earlier), axis=0, keepdims=True))
        earlier = earlier + jnp.sum(block, axis=1, keepdims=True)
    rank = jnp.concatenate(ranks, axis=1).astype(jnp.int32)
    eight = iota((8, points), 0)
    first, second, third = eight == rank, eight + 8 == rank, (eight & 3) + 16 == rank
    halves = [two_parts(w) for w in words]
    sides = []
    for side in (0, 1):
        groups = []
        for a, b in ((0, 1), (2, 3), (4, 5)):
            one, two = halves[a][side], halves[b][side]
            groups += [
                jnp.where(first, one, 0.0),
                jnp.where(second, one, 0.0),
                jnp.where(third, jnp.where(eight < 4, one, two), 0.0),
                jnp.where(first, two, 0.0),
                jnp.where(second, two, 0.0),
            ]
        groups.append(jnp.zeros((8, points), F32))
        sides.append(jnp.concatenate(groups, axis=0).astype(BF16))
    packed = lax.dot_general(
        tiles16,
        jnp.concatenate(sides, axis=0),
        (((1,), (1,)), ((), ())),
        preferred_element_type=F32,
    )
    return packed[:, :128] + packed[:, 128:]


def spread(block_ref, lhs_ref, rhs_ref):
    row_iota, lane_iota = iota((32, 128), 0), iota((256, 128), 0)
    for slot in range(SLOTS):
        where = word_row(5, slot)
        target = block_ref[where : where + 1, :].astype(jnp.int32)
        row = (target >> 7) & 31
        lane = (target & 127) | ((target >> 12) << 7)
        row_mask = row_iota == row
        columns = slice(128 * slot, 128 * slot + 128)
        rhs_ref[:, columns] = onehot(lane_iota == lane)
        for f in range(5):
            at = word_row(f, slot)
            high, low = two_parts(block_ref[at : at + 1, :])
            lhs_ref[32 * f : 32 * f + 32, columns] = jnp.where(
                row_mask, high, 0.0
            ).astype(BF16)
            lhs_ref[160 + 32 * f : 192 + 32 * f, columns] = jnp.where(
                row_mask, low, 0.0
            ).astype(BF16)


def differences(at):
    return (
        45.0 * (at(1) - at(-1)) - 9.0 * (at(2) - at(-2)) + (at(3) - at(-3))
    ) * (1.0 / 60.0)


def kernel(
    adjoint_ref,
    flow_ref,
    cell_ref,
    dest_ref,
    target_ref,
    weight_ref,
    count_ref,
    out_ref,
    packed_ref,
    plane_ref,
    near_ref,
    turned_ref,
    lhs_ref,
    rhs_ref,
    x_ref,
    y_ref,
    swap_ref,
    plane_send,
    plane_recv,
    near_send,
    near_recv,
    halo_send,
    halo_recv,
):
    sec, gx, gy = lax.axis_index("sec"), lax.axis_index("gx"), lax.axis_index("gy")
    n_gx, n_gy = lax.axis_size("gx"), lax.axis_size("gy")
    y, z = gx // NZ_DEV, gx % NZ_DEV
    me = y * NX_DEV + gy
    is_far = sec < FAR

    def plane_peer(step):
        q = (me + step) % PLANE
        return q, {"gx": (q // NX_DEV) * NZ_DEV + z, "gy": q % NX_DEV}

    def column(section, z_to):
        return {"sec": section, "gx": y * NZ_DEV + z_to, "gy": gy}

    neighbours = (
        (gx > 0, {"gx": gx - 1}),
        (gx < n_gx - 1, {"gx": gx + 1}),
        (gy > 0, {"gy": gy - 1}),
        (gy < n_gy - 1, {"gy": gy + 1}),
    )

    barrier = pltpu.get_barrier_semaphore()
    expected = jnp.where(is_far, PLANE - 1 + NZ_DEV, 0)
    for exists, device in neighbours:
        expected = expected + jnp.where(exists, 1, 0)

        @pl.when(exists)
        def _(device=device):
            pl.semaphore_signal(barrier, inc=1, device_id=device)

    @pl.when(is_far)
    def _():
        @pl.loop(1, PLANE)
        def _(step):
            pl.semaphore_signal(barrier, inc=1, device_id=plane_peer(step)[1])

    @pl.when(jnp.logical_not(is_far))
    def _():
        @pl.loop(0, FAR * NZ_DEV)
        def _(i):
            pl.semaphore_signal(
                barrier, inc=1, device_id=column(i // NZ_DEV, i % NZ_DEV)
            )

    @pl.when(is_far)
    def _():
        packed_ref[...] = pack(
            adjoint_ref[...],
            cell_ref[...],
            dest_ref[...],
            target_ref[...],
            weight_ref[...],
            count_ref[0, 0],
        )

    pl.semaphore_wait(barrier, expected)

    def own_copy():
        return pltpu.make_async_copy(
            packed_ref.at[pl.ds(pl.multiple_of(me * 8, 8), 8)],
            plane_ref.at[:, me],
            plane_recv,
        )

    def plane_copy(step):
        q, device = plane_peer(step)
        return pltpu.make_async_remote_copy(
            src_ref=packed_ref.at[pl.ds(pl.multiple_of(q * 8, 8), 8)],
            dst_ref=plane_ref.at[:, me],
            send_sem=plane_send,
            recv_sem=plane_recv,
            device_id=device,
        )

    def near_copy(step):
        z_to = (z + step) % NZ_DEV
        return pltpu.make_async_remote_copy(
            src_ref=plane_ref.at[z_to],
            dst_ref=near_ref.at[sec, z],
            send_sem=near_send,
            recv_sem=near_recv.at[sec],
            device_id=column(FAR, z_to),
        )

    @pl.when(is_far)
    def _():
        own_copy().start()

        @pl.loop(1, PLANE)
        def _(step):
            plane_copy(step).start()

    a = [adjoint_ref[64 * f : 64 * f + 64, :] for f in range(5)]
    density, m1, m2, m3, energy, sponge = (
        flow_ref[64 * f : 64 * f + 64, :] for f in range(6)
    )
    inverse = 1.0 / density
    velocity = [m * inverse for m in (m1, m2, m3)]
    kinetic = 0.5 * (m1 * m1 + m2 * m2 + m3 * m3) * inverse
    stiffness = GAMMA_RATIO * (GAMMA_MINUS * (energy - kinetic))
    pressure_like = density * a[0] + stiffness * a[4]

    def flux(direction):
        f = [velocity[direction] * a[i] for i in range(5)]
        f[1 + direction] = f[1 + direction] + pressure_like
        f[4] = f[4] + a[1 + direction] * inverse
        return f

    for f, value in enumerate(flux(0)):
        x_ref[f, 3:11] = value.reshape(8, 8, 128)
    for f, value in enumerate(flux(1)):
        swap_ref[64 * f : 64 * f + 64, :] = value
    for f in range(5):
        for j in range(8):
            y_ref[f, 3 + j] = swap_ref[pl.ds(64 * f + j, 8, stride=8), :]

    halos = []
    for ref, low, high in ((x_ref, 0, 1), (y_ref, 2, 3)):
        halos.append((ref, low, 3, 11, high))
        halos.append((ref, high, 8, 0, low))

    def halo_copy(i):
        ref, side, first, there, _ = halos[i]
        return pltpu.make_async_remote_copy(
            src_ref=ref.at[:, pl.ds(first, 3)],
            dst_ref=ref.at[:, pl.ds(there, 3)],
            send_sem=halo_send.at[i],
            recv_sem=halo_recv.at[i],
            device_id=neighbours[side][1],
        )

    for i in range(4):
        ref, side, _, there, other = halos[i]

        @pl.when(neighbours[side][0])
        def _(i=i):
            halo_copy(i).start()

        @pl.when(jnp.logical_not(neighbours[other][0]))
        def _(ref=ref, there=there):
            ref[:, there : there + 3] = jnp.zeros((5, 3, 8, 128), F32)

    @pl.when(is_far)
    def _():
        pltpu.make_async_copy(plane_ref, plane_ref, plane_recv).wait()

        @pl.loop(0, NZ_DEV)
        def _(step):
            near_copy(step).start()

    flux_z = flux(2)
    rates = []
    for f in range(5):
        value = flux_z[f]
        rates.append(
            differences(lambda o: pltpu.roll(value, (-o) % 128, 1))
        )

    for i in range(4):
        _, side, _, _, other = halos[i]

        @pl.when(neighbours[other][0])
        def _(i=i):
            halo_copy(i).wait_recv()

        @pl.when(neighbours[side][0])
        def _(i=i):
            halo_copy(i).wait_send()

    for f in range(5):
        along_y = differences(lambda o: y_ref[f, 3 + o : 11 + o])
        swap_ref[64 * f : 64 * f + 64, :] = along_y.reshape(64, 128)
    for f in range(5):
        along_x = differences(lambda o: x_ref[f, 3 + o : 11 + o]).reshape(64, 128)
        along_y = jnp.concatenate(
            [swap_ref[pl.ds(64 * f + j, 8, stride=8), :] for j in range(8)], axis=0
        )
        rate = along_x + along_y + rates[f]
        out_ref[64 * f : 64 * f + 64, :] = a[f] + STEP_SIZE * (rate - sponge * a[f])

    @pl.when(jnp.logical_not(is_far))
    def _():
        @pl.loop(0, FAR)
        def _(i):
            section = FAR - 1 - i
            pltpu.make_async_copy(
                near_ref.at[section], near_ref.at[section], near_recv.at[section]
            ).wait()
            turned_ref[...] = near_ref[section].reshape(128, 128).T
            spread(turned_ref, lhs_ref, rhs_ref)
            total = lax.dot_general(
                lhs_ref[...],
                rhs_ref[...],
                (((1,), (1,)), ((), ())),
                preferred_element_type=F32,
            )
            total = STEP_SIZE * (total[:160] + total[160:])
            for f in range(5):
                part = total[32 * f : 32 * f + 32]
                out_ref[64 * f : 64 * f + 32, :] += part[:, :128]
                out_ref[64 * f + 32 : 64 * f + 64, :] += part[:, 128:]

    @pl.when(is_far)
    def _():
        pltpu.make_async_copy(
            packed_ref.at[pl.ds(0, 8 * (PLANE - 1))],
            packed_ref.at[pl.ds(0, 8 * (PLANE - 1))],
            plane_send,
        ).wait()
        pltpu.make_async_copy(plane_ref, plane_ref, near_send).wait()


def local(adjoint, flow, point_cell, point_dest, point_target, point_weight, point_count):
    points = point_cell.shape[-1]
    vmem = pl.BlockSpec(memory_space=pltpu.VMEM)
    out = pl.pallas_call(
        kernel,
        out_shape=jax.ShapeDtypeStruct((320, 128), F32),
        in_specs=[vmem] * 6 + [pl.BlockSpec(memory_space=pltpu.SMEM)],
        out_specs=vmem,
        scratch_shapes=[
            pltpu.VMEM((128, 128), F32),
            pltpu.VMEM((NZ_DEV, PLANE, 128), F32),
            pltpu.VMEM((FAR, NZ_DEV, PLANE, 128), F32),
            pltpu.VMEM((128, 128), F32),
            pltpu.VMEM((320, SLOTS * 128), BF16),
            pltpu.VMEM((256, SLOTS * 128), BF16),
            pltpu.VMEM((5, 14, 8, 128), F32),
            pltpu.VMEM((5, 14, 8, 128), F32),
            pltpu.VMEM((320, 128), F32),
            pltpu.SemaphoreType.DMA,
            pltpu.SemaphoreType.DMA,
            pltpu.SemaphoreType.DMA,
            pltpu.SemaphoreType.DMA((FAR,)),
            pltpu.SemaphoreType.DMA((4,)),
            pltpu.SemaphoreType.DMA((4,)),
        ],
        compiler_params=pltpu.CompilerParams(
            collective_id=0, has_side_effects=True, vmem_limit_bytes=40 * 2**20
        ),
    )(
        adjoint.reshape(320, 128),
        flow.reshape(384, 128),
        point_cell.reshape(1, points),
        point_dest.reshape(1, points),
        point_target.reshape(1, points),
        point_weight.reshape(1, points),
        point_count.reshape(1, 1),
    )
    return out.reshape(1, 5, 8, 8, 128)


def solution(mesh):
    placed = (
        P("sec", None, "gx", "gy", None),
        P("sec", None, "gx", "gy", None),
        P("sec", "gx", "gy", None),
        P("sec", "gx", "gy", None),
        P("sec", "gx", "gy", None),
        P("sec", "gx", "gy", None),
        P("sec", "gx", "gy"),
    )
    return jax.shard_map(
        local,
        mesh=mesh,
        in_specs=placed,
        out_specs=P("sec", None, "gx", "gy", None),
        check_vma=False,
    )
```

```python
import jax
import jax.numpy as jnp
from jax import lax
from jax.experimental import pallas as pl
from jax.experimental.pallas import tpu as pltpu
from jax.sharding import PartitionSpec as P

GAMMA_MINUS = 0.4
GAMMA_RATIO = 1.4
STEP_SIZE = 0.4
FAR = 3
NZ_DEV = 8
NY_DEV = 4
NX_DEV = 4
PLANE = NY_DEV * NX_DEV
SLOTS = 20
VMEM_BYTES = 40 * 1024 * 1024
F32 = jnp.float32
BF16 = jnp.bfloat16


def iota(shape, dim):
    return lax.broadcasted_iota(jnp.int32, shape, dim)


def two_parts(x):
    high = x.astype(BF16).astype(F32)
    return high, (x - high).astype(BF16).astype(F32)


def onehot(condition):
    return jnp.where(condition, 1.0, 0.0).astype(BF16)


def word_row(word, slot):
    base = 40 * (word // 2)
    return base + slot if word % 2 == 0 else base + 20 + (slot + 4) % 20


def pack(adjoint, cell, dest, target, weight, count):
    points = cell.shape[1]
    live = iota((1, points), 1) < count
    row, lane = cell >> 7, cell & 127
    lanes = onehot(iota((128, points), 0) == lane)
    high, low = two_parts(adjoint)
    parts = jnp.concatenate([high.astype(BF16), low.astype(BF16)], axis=1)
    picked = jnp.dot(
        parts, jnp.concatenate([lanes, lanes], axis=0), preferred_element_type=F32
    )
    row_mask = iota((64, points), 0) == row
    scale = jnp.where(live, weight, 0.0)
    words = [
        jnp.sum(
            jnp.where(row_mask, picked[64 * f : 64 * f + 64], 0.0),
            axis=0,
            keepdims=True,
        )
        * scale
        for f in range(5)
    ]
    words.append(target.astype(F32))
    place = ((dest & 3) << 5) | ((dest >> 5) << 3) | ((dest >> 2) & 7)
    place = jnp.where(live, place, -1)
    tiles = jnp.where(iota((128, points), 0) == place, 1.0, 0.0)
    tiles16 = tiles.astype(BF16)
    before = onehot(iota((256, 256), 0) < iota((256, 256), 1))
    ranks = []
    earlier = jnp.zeros((128, 1), F32)
    for b in range(points // 256):
        block = tiles[:, 256 * b : 256 * b + 256]
        counts = jnp.dot(
            tiles16[:, 256 * b : 256 * b + 256], before, preferred_element_type=F32
        )
        ranks.append(jnp.sum(block * (counts + earlier), axis=0, keepdims=True))
        earlier = earlier + jnp.sum(block, axis=1, keepdims=True)
    rank = jnp.concatenate(ranks, axis=1).astype(jnp.int32)
    eight = iota((8, points), 0)
    first, second, third = eight == rank, eight + 8 == rank, (eight & 3) + 16 == rank
    halves = [two_parts(w) for w in words]
    sides = []
    for side in (0, 1):
        groups = []
        for a, b in ((0, 1), (2, 3), (4, 5)):
            one, two = halves[a][side], halves[b][side]
            groups += [
                jnp.where(first, one, 0.0),
                jnp.where(second, one, 0.0),
                jnp.where(third, jnp.where(eight < 4, one, two), 0.0),
                jnp.where(first, two, 0.0),
                jnp.where(second, two, 0.0),
            ]
        groups.append(jnp.zeros((8, points), F32))
        sides.append(jnp.concatenate(groups, axis=0).astype(BF16))
    packed = lax.dot_general(
        tiles16,
        jnp.concatenate(sides, axis=0),
        (((1,), (1,)), ((), ())),
        preferred_element_type=F32,
    )
    return packed[:, :128] + packed[:, 128:]


def spread(block_ref, lhs_ref, rhs_ref):
    row_iota, lane_iota = iota((32, 128), 0), iota((256, 128), 0)
    for slot in range(SLOTS):
        where = word_row(5, slot)
        target = block_ref[where : where + 1, :].astype(jnp.int32)
        row = (target >> 7) & 31
        lane = (target & 127) | ((target >> 12) << 7)
        row_mask = row_iota == row
        columns = slice(128 * slot, 128 * slot + 128)
        rhs_ref[:, columns] = onehot(lane_iota == lane)
        for f in range(5):
            at = word_row(f, slot)
            high, low = two_parts(block_ref[at : at + 1, :])
            lhs_ref[32 * f : 32 * f + 32, columns] = jnp.where(
                row_mask, high, 0.0
            ).astype(BF16)
            lhs_ref[160 + 32 * f : 192 + 32 * f, columns] = jnp.where(
                row_mask, low, 0.0
            ).astype(BF16)


def differences(at):
    return (
        45.0 * (at(1) - at(-1)) - 9.0 * (at(2) - at(-2)) + (at(3) - at(-3))
    ) * (1.0 / 60.0)


def kernel(
    adjoint_hbm,
    flow_hbm,
    cell_hbm,
    dest_hbm,
    target_hbm,
    weight_hbm,
    count_hbm,
    out_ref,
    adjoint_ref,
    flow_ref,
    cell_ref,
    dest_ref,
    target_ref,
    weight_ref,
    count_ref,
    packed_ref,
    x_stage_ref,
    y_stage_ref,
    column_ref,
    near_ref,
    turned_ref,
    lhs_ref,
    rhs_ref,
    x_ref,
    y_ref,
    swap_ref,
    in_sem,
    close_sem,
    wide_sem,
    x_send,
    x_recv,
    y_send,
    y_recv,
    near_send,
    near_recv,
    halo_send,
    halo_recv,
):
    loads = [
        pltpu.make_async_copy(src, dst, in_sem.at[i])
        for i, (src, dst) in enumerate(
            (
                (adjoint_hbm, adjoint_ref),
                (flow_hbm, flow_ref),
                (cell_hbm, cell_ref),
                (dest_hbm, dest_ref),
                (target_hbm, target_ref),
                (weight_hbm, weight_ref),
                (count_hbm, count_ref),
            )
        )
    ]
    for load in loads:
        load.start()

    sec, gx, gy = lax.axis_index("sec"), lax.axis_index("gx"), lax.axis_index("gy")
    n_gx, n_gy = lax.axis_size("gx"), lax.axis_size("gy")
    y, z = gx // NZ_DEV, gx % NZ_DEV
    is_far = sec < FAR
    is_near = sec == FAR
    core = sec % 2
    first_core = sec - core
    low_half = sec < 2

    barrier = pltpu.get_barrier_semaphore()

    def tell(condition, device):
        @pl.when(condition)
        def _():
            pl.semaphore_signal(barrier, inc=1, device_id=device)

    one, zero = jnp.int32(1), jnp.int32(0)

    def number(condition):
        return jnp.where(condition, one, zero)

    has_low, has_high = gx > 0, gx < n_gx - 1
    neighbours = (
        (has_low, {"gx": gx - 1}),
        (has_high, {"gx": gx + 1}),
        (gy > 0, {"gy": gy - 1}),
        (gy < n_gy - 1, {"gy": gy + 1}),
    )
    tell(has_low, {"sec": first_core, "gx": gx - 1})
    tell(has_high & (z < NZ_DEV - 1), {"sec": first_core, "gx": gx + 1})
    tell(has_high & (z == NZ_DEV - 1), {"sec": first_core + 1, "gx": gx + 1})
    tell(gy > 0, {"sec": first_core, "gy": gy - 1})
    tell(gy < n_gy - 1, {"sec": first_core, "gy": gy + 1})
    tell(core == 1, {"sec": first_core})
    tell(core == 0, {"sec": first_core + 1})

    def x_peer(step):
        to = (gy + step) % NX_DEV
        return to, {"gy": to}

    def y_peer(step):
        to = (y + step) % NY_DEV
        return to, {"gx": to * NZ_DEV + z}

    @pl.when(is_far)
    def _():
        for step in (1, 2, 3):
            for _, device in (x_peer(step), y_peer(step)):
                pl.semaphore_signal(
                    barrier, inc=1, device_id={"sec": first_core, **device}
                )

    @pl.when(is_near)
    def _():
        @pl.loop(0, NZ_DEV)
        def _(i):
            to = {"sec": 1, "gx": y * NZ_DEV + (z + i) % NZ_DEV}
            pl.semaphore_signal(barrier, inc=1, device_id=to)

        @pl.loop(1, NZ_DEV)
        def _(i):
            to = {"gx": y * NZ_DEV + (z + i) % NZ_DEV}
            pl.semaphore_signal(barrier, inc=1, device_id=to)

    close_count = (
        2
        * (
            number(has_low & (z > 0))
            + number(has_high)
            + number(gy > 0)
            + number(gy < n_gy - 1)
        )
        + jnp.where(low_half, 12, 6)
        + 1
    )
    wide_count = jnp.where(low_half, 8, 7) + 2 * number(has_low & (z == 0)) + 1

    for load in loads:
        load.wait()

    @pl.when(is_far)
    def _():
        packed_ref[...] = pack(
            adjoint_ref[...],
            cell_ref[...],
            dest_ref[...],
            target_ref[...],
            weight_ref[...],
            count_ref[0, 0, 0],
        ).reshape(4, 4, 8, 128)

    a = [adjoint_ref[64 * f : 64 * f + 64, :] for f in range(5)]
    density, m1, m2, m3, energy, sponge = (
        flow_ref[64 * f : 64 * f + 64, :] for f in range(6)
    )
    inverse = 1.0 / density
    velocity = [m * inverse for m in (m1, m2, m3)]
    kinetic = 0.5 * (m1 * m1 + m2 * m2 + m3 * m3) * inverse
    stiffness = GAMMA_RATIO * (GAMMA_MINUS * (energy - kinetic))
    pressure_like = density * a[0] + stiffness * a[4]

    def flux(direction):
        f = [velocity[direction] * a[i] for i in range(5)]
        f[1 + direction] = f[1 + direction] + pressure_like
        f[4] = f[4] + a[1 + direction] * inverse
        return f

    for f, value in enumerate(flux(0)):
        x_ref[f, 3:11] = value.reshape(8, 8, 128)
    for f, value in enumerate(flux(1)):
        swap_ref[64 * f : 64 * f + 64, :] = value
    for f in range(5):
        for j in range(8):
            y_ref[f, 3 + j] = swap_ref[pl.ds(64 * f + j, 8, stride=8), :]

    @pl.when(core == 0)
    def _():
        pl.semaphore_wait(barrier, close_count)
        pl.semaphore_signal(close_sem, inc=1, device_id={"sec": first_core + 1})

    @pl.when(core == 1)
    def _():
        pl.semaphore_wait(close_sem, 1)

    halos = []
    for ref, low, high in ((x_ref, 0, 1), (y_ref, 2, 3)):
        halos.append((ref, low, 3, 11, high))
        halos.append((ref, high, 8, 0, low))

    def halo_copy(i):
        ref, side, first, there, _ = halos[i]
        return pltpu.make_async_remote_copy(
            src_ref=ref.at[:, pl.ds(first, 3)],
            dst_ref=ref.at[:, pl.ds(there, 3)],
            send_sem=halo_send.at[i],
            recv_sem=halo_recv.at[i],
            device_id=neighbours[side][1],
        )

    def own_x_copy():
        return pltpu.make_async_copy(
            packed_ref.at[gy], x_stage_ref.at[gy], x_recv
        )

    def x_copy(step):
        to, device = x_peer(step)
        return pltpu.make_async_remote_copy(
            src_ref=packed_ref.at[to],
            dst_ref=x_stage_ref.at[gy],
            send_sem=x_send,
            recv_sem=x_recv,
            device_id=device,
        )

    def own_y_copy():
        return pltpu.make_async_copy(
            x_stage_ref.at[:, y], y_stage_ref.at[y], y_recv
        )

    def y_copy(step):
        to, device = y_peer(step)
        return pltpu.make_async_remote_copy(
            src_ref=x_stage_ref.at[:, to],
            dst_ref=y_stage_ref.at[y],
            send_sem=y_send,
            recv_sem=y_recv,
            device_id=device,
        )

    def near_copy(step):
        z_to = (z + step) % NZ_DEV
        return pltpu.make_async_remote_copy(
            src_ref=column_ref.at[z_to],
            dst_ref=near_ref.at[sec, z],
            send_sem=near_send,
            recv_sem=near_recv.at[sec],
            device_id={"sec": FAR, "gx": y * NZ_DEV + z_to},
        )

    @pl.when(is_far)
    def _():
        for step in (1, 2, 3):
            x_copy(step).start()
        own_x_copy().start()

    for i in (1, 0, 2, 3):
        ref, side, _, there, other = halos[i]
        now = neighbours[side][0]
        if i == 0:
            now = now & (z > 0)

        @pl.when(now)
        def _(i=i):
            halo_copy(i).start()

        @pl.when(jnp.logical_not(neighbours[other][0]))
        def _(ref=ref, there=there):
            ref[:, there : there + 3] = jnp.zeros((5, 3, 8, 128), F32)

    flux_z = flux(2)
    for f in range(5):
        value = flux_z[f]
        along_z = differences(lambda o: pltpu.roll(value, (-o) % 128, 1))
        out_ref[64 * f : 64 * f + 64, :] = a[f] + STEP_SIZE * (along_z - sponge * a[f])

    @pl.when(is_far)
    def _():
        pltpu.make_async_copy(x_stage_ref, x_stage_ref, x_recv).wait()
        for step in (1, 2, 3):
            y_copy(step).start()
        own_y_copy().start()

    def add_x(first, last):
        rows = 8 * (last - first)
        for f in range(5):
            along_x = differences(lambda o: x_ref[f, 3 + first + o : 3 + last + o])
            at = 64 * f + 8 * first
            out_ref[at : at + rows, :] += STEP_SIZE * along_x.reshape(rows, 128)

    add_x(3, 5)

    @pl.when(is_far)
    def _():
        pltpu.make_async_copy(y_stage_ref, y_stage_ref, y_recv).wait()
        for to in range(NZ_DEV):
            for x_from in range(NX_DEV):
                column_ref[to, 4 * x_from : 4 * x_from + 4] = y_stage_ref[
                    :, x_from, to, :
                ]

    @pl.when(core == 1)
    def _():
        pl.semaphore_wait(barrier, wide_count)
        pl.semaphore_signal(wide_sem, inc=1, device_id={"sec": first_core})

    @pl.when(core == 0)
    def _():
        pl.semaphore_wait(wide_sem, 1)

    @pl.when(has_low & (z == 0))
    def _():
        halo_copy(0).start()

    @pl.when(is_far)
    def _():
        @pl.loop(0, NZ_DEV)
        def _(step):
            near_copy(step).start()

    def receive(i):
        @pl.when(neighbours[halos[i][4]][0])
        def _():
            halo_copy(i).wait_recv()

    receive(2)
    receive(3)
    for f in range(5):
        along_y = differences(lambda o: y_ref[f, 3 + o : 11 + o])
        swap_ref[64 * f : 64 * f + 64, :] = along_y.reshape(64, 128)
    for f in range(5):
        for j in range(8):
            at = 64 * f + 8 * j
            out_ref[at : at + 8, :] += (
                STEP_SIZE * swap_ref[pl.ds(64 * f + j, 8, stride=8), :]
            )
    receive(0)
    add_x(5, 8)
    receive(1)
    add_x(0, 3)

    @pl.when(is_near)
    def _():
        @pl.loop(0, FAR)
        def _(i):
            section = FAR - 1 - i
            pltpu.make_async_copy(
                near_ref.at[section], near_ref.at[section], near_recv.at[section]
            ).wait()
            turned_ref[...] = near_ref[section].reshape(128, 128).T
            spread(turned_ref, lhs_ref, rhs_ref)
            total = lax.dot_general(
                lhs_ref[...],
                rhs_ref[...],
                (((1,), (1,)), ((), ())),
                preferred_element_type=F32,
            )
            total = STEP_SIZE * (total[:160] + total[160:])
            for f in range(5):
                part = total[32 * f : 32 * f + 32]
                out_ref[64 * f : 64 * f + 32, :] += part[:, :128]
                out_ref[64 * f + 32 : 64 * f + 64, :] += part[:, 128:]

    for i in range(4):

        @pl.when(neighbours[halos[i][1]][0])
        def _(i=i):
            halo_copy(i).wait_send()

    @pl.when(is_far)
    def _():
        three = packed_ref.at[pl.ds(0, 3)]
        pltpu.make_async_copy(three, three, x_send).wait()
        pltpu.make_async_copy(three, three, y_send).wait()
        pltpu.make_async_copy(column_ref, column_ref, near_send).wait()


def local(adjoint, flow, point_cell, point_dest, point_target, point_weight, point_count):
    points = point_cell.shape[-1]
    hbm = pl.BlockSpec(memory_space=pl.ANY)
    out = pl.pallas_call(
        kernel,
        out_shape=jax.ShapeDtypeStruct((320, 128), F32),
        in_specs=[hbm] * 7,
        out_specs=pl.BlockSpec(memory_space=pltpu.VMEM),
        scratch_shapes=[
            pltpu.VMEM((320, 128), F32),
            pltpu.VMEM((384, 128), F32),
            pltpu.VMEM((1, points), jnp.int32),
            pltpu.VMEM((1, points), jnp.int32),
            pltpu.VMEM((1, points), jnp.int32),
            pltpu.VMEM((1, points), F32),
            pltpu.SMEM((1, 1, 1), jnp.int32),
            pltpu.VMEM((NX_DEV, NY_DEV, NZ_DEV, 128), F32),
            pltpu.VMEM((NX_DEV, NY_DEV, NZ_DEV, 128), F32),
            pltpu.VMEM((NY_DEV, NX_DEV, NZ_DEV, 128), F32),
            pltpu.VMEM((NZ_DEV, PLANE, 128), F32),
            pltpu.VMEM((FAR, NZ_DEV, PLANE, 128), F32),
            pltpu.VMEM((128, 128), F32),
            pltpu.VMEM((320, SLOTS * 128), BF16),
            pltpu.VMEM((256, SLOTS * 128), BF16),
            pltpu.VMEM((5, 14, 8, 128), F32),
            pltpu.VMEM((5, 14, 8, 128), F32),
            pltpu.VMEM((320, 128), F32),
            pltpu.SemaphoreType.DMA((7,)),
            pltpu.SemaphoreType.REGULAR,
            pltpu.SemaphoreType.REGULAR,
            pltpu.SemaphoreType.DMA,
            pltpu.SemaphoreType.DMA,
            pltpu.SemaphoreType.DMA,
            pltpu.SemaphoreType.DMA,
            pltpu.SemaphoreType.DMA,
            pltpu.SemaphoreType.DMA((FAR,)),
            pltpu.SemaphoreType.DMA((4,)),
            pltpu.SemaphoreType.DMA((4,)),
        ],
        compiler_params=pltpu.CompilerParams(
            collective_id=0, has_side_effects=True, vmem_limit_bytes=VMEM_BYTES
        ),
    )(
        adjoint.reshape(320, 128),
        flow.reshape(384, 128),
        point_cell.reshape(1, points),
        point_dest.reshape(1, points),
        point_target.reshape(1, points),
        point_weight.reshape(1, points),
        point_count,
    )
    return out.reshape(1, 5, 8, 8, 128)


def solution(mesh):
    placed = (
        P("sec", None, "gx", "gy", None),
        P("sec", None, "gx", "gy", None),
        P("sec", "gx", "gy", None),
        P("sec", "gx", "gy", None),
        P("sec", "gx", "gy", None),
        P("sec", "gx", "gy", None),
        P("sec", "gx", "gy"),
    )
    return jax.shard_map(
        local,
        mesh=mesh,
        in_specs=placed,
        out_specs=P("sec", None, "gx", "gy", None),
        check_vma=False,
    )
```

```python
import jax
import jax.numpy as jnp
from jax import lax
from jax.experimental import pallas as pl
from jax.experimental.pallas import tpu as pltpu
from jax.sharding import PartitionSpec as P

GAMMA_MINUS = 0.4
GAMMA_RATIO = 1.4
STEP_SIZE = 0.4
FAR = 3
NZ_DEV = 8
NY_DEV = 4
NX_DEV = 4
PLANE = NY_DEV * NX_DEV
SLOTS = 20
VMEM_BYTES = 55000 * 1024
F32 = jnp.float32
BF16 = jnp.bfloat16


def iota(shape, dim):
    return lax.broadcasted_iota(jnp.int32, shape, dim)


def two_parts(x):
    high = x.astype(BF16).astype(F32)
    return high, (x - high).astype(BF16).astype(F32)


def onehot(condition):
    return jnp.where(condition, 1.0, 0.0).astype(BF16)


def word_row(word, slot):
    base = 40 * (word // 2)
    return base + slot if word % 2 == 0 else base + 20 + (slot + 4) % 20


def pack(adjoint, cell, dest, target, weight, count):
    points = cell.shape[1]
    live = iota((1, points), 1) < count
    row, lane = cell >> 7, cell & 127
    lanes = onehot(iota((128, points), 0) == lane)
    high, low = two_parts(adjoint)
    parts = jnp.concatenate([high.astype(BF16), low.astype(BF16)], axis=1)
    picked = jnp.dot(
        parts, jnp.concatenate([lanes, lanes], axis=0), preferred_element_type=F32
    )
    row_mask = iota((64, points), 0) == row
    scale = jnp.where(live, weight, 0.0)
    words = [
        jnp.sum(
            jnp.where(row_mask, picked[64 * f : 64 * f + 64], 0.0),
            axis=0,
            keepdims=True,
        )
        * scale
        for f in range(5)
    ]
    words.append(target.astype(F32))
    place = (dest & 96) | ((dest & 3) << 3) | ((dest >> 2) & 7)
    place = jnp.where(live, place, -1)
    tiles = jnp.where(iota((128, points), 0) == place, 1.0, 0.0)
    tiles16 = tiles.astype(BF16)
    before = onehot(iota((256, 256), 0) < iota((256, 256), 1))
    ranks = []
    earlier = jnp.zeros((128, 1), F32)
    for b in range(points // 256):
        block = tiles[:, 256 * b : 256 * b + 256]
        counts = jnp.dot(
            tiles16[:, 256 * b : 256 * b + 256], before, preferred_element_type=F32
        )
        ranks.append(jnp.sum(block * (counts + earlier), axis=0, keepdims=True))
        earlier = earlier + jnp.sum(block, axis=1, keepdims=True)
    rank = jnp.concatenate(ranks, axis=1).astype(jnp.int32)
    eight = iota((8, points), 0)
    first, second, third = eight == rank, eight + 8 == rank, (eight & 3) + 16 == rank
    halves = [two_parts(w) for w in words]
    sides = []
    for side in (0, 1):
        groups = []
        for a, b in ((0, 1), (2, 3), (4, 5)):
            one, two = halves[a][side], halves[b][side]
            groups += [
                jnp.where(first, one, 0.0),
                jnp.where(second, one, 0.0),
                jnp.where(third, jnp.where(eight < 4, one, two), 0.0),
                jnp.where(first, two, 0.0),
                jnp.where(second, two, 0.0),
            ]
        groups.append(jnp.zeros((8, points), F32))
        sides.append(jnp.concatenate(groups, axis=0).astype(BF16))
    packed = lax.dot_general(
        tiles16,
        jnp.concatenate(sides, axis=0),
        (((1,), (1,)), ((), ())),
        preferred_element_type=F32,
    )
    return packed[:, :128] + packed[:, 128:]


def spread(block_ref, lhs_ref, rhs_ref):
    row_iota, lane_iota = iota((32, 128), 0), iota((256, 128), 0)
    for slot in range(SLOTS):
        where = word_row(5, slot)
        target = block_ref[where : where + 1, :].astype(jnp.int32)
        row = (target >> 7) & 31
        lane = (target & 127) | ((target >> 12) << 7)
        row_mask = row_iota == row
        columns = slice(128 * slot, 128 * slot + 128)
        rhs_ref[:, columns] = onehot(lane_iota == lane)
        for f in range(5):
            at = word_row(f, slot)
            high, low = two_parts(block_ref[at : at + 1, :])
            lhs_ref[32 * f : 32 * f + 32, columns] = jnp.where(
                row_mask, high, 0.0
            ).astype(BF16)
            lhs_ref[160 + 32 * f : 192 + 32 * f, columns] = jnp.where(
                row_mask, low, 0.0
            ).astype(BF16)


def differences(at):
    return (
        45.0 * (at(1) - at(-1)) - 9.0 * (at(2) - at(-2)) + (at(3) - at(-3))
    ) * (1.0 / 60.0)


def kernel(
    adjoint_hbm,
    flow_hbm,
    cell_hbm,
    dest_hbm,
    target_hbm,
    weight_hbm,
    count_hbm,
    out_ref,
    adjoint_ref,
    flow_ref,
    cell_ref,
    dest_ref,
    target_ref,
    weight_ref,
    count_ref,
    packed_ref,
    plane_ref,
    column_ref,
    near_ref,
    turned_ref,
    lhs_ref,
    rhs_ref,
    x_ref,
    y_ref,
    swap_ref,
    in_sem,
    turn_sem,
    close_sem,
    wide_sem,
    plane_send,
    plane_recv,
    near_send,
    near_recv,
    halo_send,
    halo_recv,
):
    loads = [
        pltpu.make_async_copy(src, dst, in_sem.at[i])
        for i, (src, dst) in enumerate(
            (
                (adjoint_hbm, adjoint_ref),
                (flow_hbm, flow_ref),
                (cell_hbm, cell_ref),
                (dest_hbm, dest_ref),
                (target_hbm, target_ref),
                (weight_hbm, weight_ref),
                (count_hbm, count_ref),
            )
        )
    ]
    for load in loads:
        load.start()

    sec, gx, gy = lax.axis_index("sec"), lax.axis_index("gx"), lax.axis_index("gy")
    n_gx, n_gy = lax.axis_size("gx"), lax.axis_size("gy")
    y, z = gx // NZ_DEV, gx % NZ_DEV
    is_far = sec < FAR
    is_near = sec == FAR
    core = sec % 2
    first_core = sec - core
    low_half = sec < 2
    me = y * NX_DEV + gy
    last_z = z == NZ_DEV - 1
    high_turn, low_turn = (gx < n_gx - 1) & last_z, (gx > 0) & (z == 0)

    barrier = pltpu.get_barrier_semaphore()

    def tell(condition, device):
        @pl.when(condition)
        def _():
            pl.semaphore_signal(barrier, inc=1, device_id=device)

    one, zero = jnp.int32(1), jnp.int32(0)

    def number(condition):
        return jnp.where(condition, one, zero)

    has_low, has_high = gx > 0, gx < n_gx - 1
    neighbours = (
        (has_low, {"gx": gx - 1}),
        (has_high, {"gx": gx + 1}),
        (gy > 0, {"gy": gy - 1}),
        (gy < n_gy - 1, {"gy": gy + 1}),
    )
    tell(has_low & (z > 0), {"sec": first_core, "gx": gx - 1})
    tell(low_turn, {"sec": first_core + 1, "gx": gx - 1})
    tell(has_high & jnp.logical_not(last_z), {"sec": first_core, "gx": gx + 1})
    tell(high_turn, {"sec": first_core + 1, "gx": gx + 1})
    tell(gy > 0, {"sec": first_core, "gy": gy - 1})
    tell(gy < n_gy - 1, {"sec": first_core, "gy": gy + 1})
    tell(core == 1, {"sec": first_core})
    tell(core == 0, {"sec": first_core + 1})
    tell(last_z, {"sec": first_core + 1, "gx": gx - 1})

    def plane_peer(step):
        q = (me + step) % PLANE
        return q, {"gx": (q // NX_DEV) * NZ_DEV + z, "gy": q % NX_DEV}

    @pl.when(is_far)
    def _():
        @pl.loop(1, PLANE)
        def _(step):
            to = {"sec": first_core, **plane_peer(step)[1]}
            pl.semaphore_signal(barrier, inc=1, device_id=to)

    @pl.when(is_near)
    def _():
        @pl.loop(0, NZ_DEV - 1)
        def _(i):
            to = {"sec": 1, "gx": y * NZ_DEV + i}
            pl.semaphore_signal(barrier, inc=1, device_id=to)

        @pl.loop(0, NZ_DEV - 1)
        def _(i):
            @pl.when(i != z)
            def _():
                to = {"gx": y * NZ_DEV + i}
                pl.semaphore_signal(barrier, inc=1, device_id=to)

    close_count = (
        2
        * (
            number(has_low & (z > 0))
            + number(has_high & jnp.logical_not(last_z))
            + number(gy > 0)
            + number(gy < n_gy - 1)
        )
        + (PLANE - 1) * jnp.where(low_half, 2, 1)
        + 1
    )
    wide_count = (
        jnp.where(low_half, NZ_DEV, NZ_DEV - 1)
        + 2 * number(low_turn)
        + 2 * number(z == NZ_DEV - 2)
        + 1
    )
    turn_count = 2 * number(high_turn) + 1

    loads[0].wait()
    loads[1].wait()

    a = [adjoint_ref[64 * f : 64 * f + 64, :] for f in range(5)]
    density, m1, m2, m3, energy, sponge = (
        flow_ref[64 * f : 64 * f + 64, :] for f in range(6)
    )
    inverse = 1.0 / density
    velocity = [m * inverse for m in (m1, m2, m3)]
    kinetic = 0.5 * (m1 * m1 + m2 * m2 + m3 * m3) * inverse
    stiffness = GAMMA_RATIO * (GAMMA_MINUS * (energy - kinetic))
    pressure_like = density * a[0] + stiffness * a[4]

    def flux(direction):
        f = [velocity[direction] * a[i] for i in range(5)]
        f[1 + direction] = f[1 + direction] + pressure_like
        f[4] = f[4] + a[1 + direction] * inverse
        return f

    for f, value in enumerate(flux(0)):
        x_ref[f, 3:11] = value.reshape(8, 8, 128)
    halos = []
    for ref, low, high in ((x_ref, 0, 1), (y_ref, 2, 3)):
        halos.append((ref, low, 3, 11, high))
        halos.append((ref, high, 8, 0, low))

    def halo_copy(i):
        ref, side, first, there, _ = halos[i]
        return pltpu.make_async_remote_copy(
            src_ref=ref.at[:, pl.ds(first, 3)],
            dst_ref=ref.at[:, pl.ds(there, 3)],
            send_sem=halo_send.at[i],
            recv_sem=halo_recv.at[i],
            device_id=neighbours[side][1],
        )

    @pl.when(last_z & (core == 1))
    def _():
        pl.semaphore_wait(barrier, turn_count)
        pl.semaphore_signal(turn_sem, inc=1, device_id={"sec": first_core})

    @pl.when(last_z & (core == 0))
    def _():
        pl.semaphore_wait(turn_sem, 1)

    @pl.when(high_turn)
    def _():
        halo_copy(1).start()

    for load in loads[2:]:
        load.wait()

    @pl.when(is_far)
    def _():
        packed_ref[...] = pack(
            adjoint_ref[...],
            cell_ref[...],
            dest_ref[...],
            target_ref[...],
            weight_ref[...],
            count_ref[0, 0, 0],
        )

    for f, value in enumerate(flux(1)):
        swap_ref[64 * f : 64 * f + 64, :] = value
    for f in range(5):
        for j in range(8):
            y_ref[f, 3 + j] = swap_ref[pl.ds(64 * f + j, 8, stride=8), :]

    @pl.when(core == 0)
    def _():
        pl.semaphore_wait(barrier, close_count)
        pl.semaphore_signal(close_sem, inc=1, device_id={"sec": first_core + 1})

    @pl.when(core == 1)
    def _():
        pl.semaphore_wait(close_sem, 1)

    def own_copy():
        return pltpu.make_async_copy(
            packed_ref.at[pl.ds(pl.multiple_of(me * 8, 8), 8)],
            plane_ref.at[me],
            plane_recv,
        )

    def plane_copy(step):
        q, device = plane_peer(step)
        return pltpu.make_async_remote_copy(
            src_ref=packed_ref.at[pl.ds(pl.multiple_of(q * 8, 8), 8)],
            dst_ref=plane_ref.at[me],
            send_sem=plane_send,
            recv_sem=plane_recv,
            device_id=device,
        )

    chunk = jnp.where(low_half, 1 + z // 4, 0)
    place = jnp.where(low_half, 4 * core + z % 4, z)

    def near_copy(step):
        z_to = (z + step) % NZ_DEV
        return pltpu.make_async_remote_copy(
            src_ref=column_ref.at[z_to],
            dst_ref=near_ref.at[chunk, place],
            send_sem=near_send,
            recv_sem=near_recv.at[chunk],
            device_id={"sec": FAR, "gx": y * NZ_DEV + z_to},
        )

    @pl.when(is_far)
    def _():
        own_copy().start()

        @pl.loop(1, PLANE)
        def _(step):
            plane_copy(step).start()

    for i in (1, 0, 2, 3):
        ref, side, _, there, other = halos[i]
        now = neighbours[side][0]
        if i == 0:
            now = now & (z > 0)
        if i == 1:
            now = now & jnp.logical_not(last_z)

        @pl.when(now)
        def _(i=i):
            halo_copy(i).start()

        @pl.when(jnp.logical_not(neighbours[other][0]))
        def _(ref=ref, there=there):
            ref[:, there : there + 3] = jnp.zeros((5, 3, 8, 128), F32)

    flux_z = flux(2)
    for f in range(5):
        value = flux_z[f]
        along_z = differences(lambda o: pltpu.roll(value, (-o) % 128, 1))
        out_ref[64 * f : 64 * f + 64, :] = a[f] + STEP_SIZE * (along_z - sponge * a[f])

    def add_x(first, last):
        rows = 8 * (last - first)
        for f in range(5):
            along_x = differences(lambda o: x_ref[f, 3 + first + o : 3 + last + o])
            at = 64 * f + 8 * first
            out_ref[at : at + rows, :] += STEP_SIZE * along_x.reshape(rows, 128)

    add_x(3, 5)

    @pl.when(is_far)
    def _():
        pltpu.make_async_copy(plane_ref, plane_ref, plane_recv).wait()
        for to in range(NZ_DEV):
            column_ref[to] = plane_ref[:, to, :]

    @pl.when((core == 1) & jnp.logical_not(last_z))
    def _():
        pl.semaphore_wait(barrier, wide_count)
        pl.semaphore_signal(wide_sem, inc=1, device_id={"sec": first_core})

        @pl.when(z == NZ_DEV - 2)
        def _():
            for to in (0, 1):
                device = {"sec": first_core + to, "gx": gx + 1}
                pl.semaphore_signal(wide_sem, inc=1, device_id=device)

    @pl.when((core == 0) | last_z)
    def _():
        pl.semaphore_wait(wide_sem, 1)

    @pl.when(low_turn)
    def _():
        halo_copy(0).start()

    @pl.when(is_far)
    def _():
        @pl.loop(0, NZ_DEV)
        def _(step):
            near_copy(step).start()

    def receive(i):
        @pl.when(neighbours[halos[i][4]][0])
        def _():
            halo_copy(i).wait_recv()

    receive(2)
    receive(3)
    for f in range(5):
        along_y = differences(lambda o: y_ref[f, 3 + o : 11 + o])
        swap_ref[64 * f : 64 * f + 64, :] = along_y.reshape(64, 128)
    for f in range(5):
        for j in range(8):
            at = 64 * f + 8 * j
            out_ref[at : at + 8, :] += (
                STEP_SIZE * swap_ref[pl.ds(64 * f + j, 8, stride=8), :]
            )
    receive(0)
    add_x(5, 8)
    receive(1)
    add_x(0, 3)

    @pl.when(is_near)
    def _():
        @pl.loop(0, FAR)
        def _(i):
            pltpu.make_async_copy(
                near_ref.at[i], near_ref.at[i], near_recv.at[i]
            ).wait()
            turned_ref[...] = near_ref[i].reshape(128, 128).T
            spread(turned_ref, lhs_ref, rhs_ref)
            total = lax.dot_general(
                lhs_ref[...],
                rhs_ref[...],
                (((1,), (1,)), ((), ())),
                preferred_element_type=F32,
            )
            total = STEP_SIZE * (total[:160] + total[160:])
            for f in range(5):
                part = total[32 * f : 32 * f + 32]
                out_ref[64 * f : 64 * f + 32, :] += part[:, :128]
                out_ref[64 * f + 32 : 64 * f + 64, :] += part[:, 128:]

    for i in range(4):

        @pl.when(neighbours[halos[i][1]][0])
        def _(i=i):
            halo_copy(i).wait_send()

    @pl.when(is_far)
    def _():
        others = packed_ref.at[pl.ds(0, 8 * (PLANE - 1))]
        pltpu.make_async_copy(others, others, plane_send).wait()
        pltpu.make_async_copy(column_ref, column_ref, near_send).wait()


def local(adjoint, flow, point_cell, point_dest, point_target, point_weight, point_count):
    points = point_cell.shape[-1]
    hbm = pl.BlockSpec(memory_space=pl.ANY)
    out = pl.pallas_call(
        kernel,
        out_shape=jax.ShapeDtypeStruct((320, 128), F32),
        in_specs=[hbm] * 7,
        out_specs=pl.BlockSpec(memory_space=pltpu.VMEM),
        scratch_shapes=[
            pltpu.VMEM((320, 128), F32),
            pltpu.VMEM((384, 128), F32),
            pltpu.VMEM((1, points), jnp.int32),
            pltpu.VMEM((1, points), jnp.int32),
            pltpu.VMEM((1, points), jnp.int32),
            pltpu.VMEM((1, points), F32),
            pltpu.SMEM((1, 1, 1), jnp.int32),
            pltpu.VMEM((128, 128), F32),
            pltpu.VMEM((PLANE, NZ_DEV, 128), F32),
            pltpu.VMEM((NZ_DEV, PLANE, 128), F32),
            pltpu.VMEM((FAR, NZ_DEV, PLANE, 128), F32),
            pltpu.VMEM((128, 128), F32),
            pltpu.VMEM((320, SLOTS * 128), BF16),
            pltpu.VMEM((256, SLOTS * 128), BF16),
            pltpu.VMEM((5, 14, 8, 128), F32),
            pltpu.VMEM((5, 14, 8, 128), F32),
            pltpu.VMEM((320, 128), F32),
            pltpu.SemaphoreType.DMA((7,)),
            pltpu.SemaphoreType.REGULAR,
            pltpu.SemaphoreType.REGULAR,
            pltpu.SemaphoreType.REGULAR,
            pltpu.SemaphoreType.DMA,
            pltpu.SemaphoreType.DMA,
            pltpu.SemaphoreType.DMA,
            pltpu.SemaphoreType.DMA((FAR,)),
            pltpu.SemaphoreType.DMA((4,)),
            pltpu.SemaphoreType.DMA((4,)),
        ],
        cost_estimate=pl.CostEstimate(
            flops=2 * 10**9, bytes_accessed=10**6, transcendentals=0
        ),
        compiler_params=pltpu.CompilerParams(
            collective_id=0, has_side_effects=True, vmem_limit_bytes=VMEM_BYTES
        ),
    )(
        adjoint.reshape(320, 128),
        flow.reshape(384, 128),
        point_cell.reshape(1, points),
        point_dest.reshape(1, points),
        point_target.reshape(1, points),
        point_weight.reshape(1, points),
        point_count,
    )
    return out.reshape(1, 5, 8, 8, 128)


def solution(mesh):
    placed = (
        P("sec", None, "gx", "gy", None),
        P("sec", None, "gx", "gy", None),
        P("sec", "gx", "gy", None),
        P("sec", "gx", "gy", None),
        P("sec", "gx", "gy", None),
        P("sec", "gx", "gy", None),
        P("sec", "gx", "gy"),
    )
    return jax.shard_map(
        local,
        mesh=mesh,
        in_specs=placed,
        out_specs=P("sec", None, "gx", "gy", None),
        check_vma=False,
    )
```

```python
import jax
import jax.numpy as jnp
from jax import lax
from jax.experimental import pallas as pl
from jax.experimental.pallas import tpu as pltpu
from jax.sharding import PartitionSpec as P

GAMMA_MINUS = 0.4
GAMMA_RATIO = 1.4
STEP_SIZE = 0.4
FAR = 3
NZ_DEV = 8
NY_DEV = 4
NX_DEV = 4
PLANE = NY_DEV * NX_DEV
SLOTS = 20
VMEM_BYTES = 40 * 1024 * 1024
F32 = jnp.float32
BF16 = jnp.bfloat16


def iota(shape, dim):
    return lax.broadcasted_iota(jnp.int32, shape, dim)


def two_parts(x):
    high = x.astype(BF16).astype(F32)
    return high, (x - high).astype(BF16).astype(F32)


def onehot(condition):
    return jnp.where(condition, 1.0, 0.0).astype(BF16)


def word_row(word, slot):
    base = 40 * (word // 2)
    return base + slot if word % 2 == 0 else base + 20 + (slot + 4) % 20


def pack(adjoint, cell, dest, target, weight, count):
    points = cell.shape[1]
    live = iota((1, points), 1) < count
    row, lane = cell >> 7, cell & 127
    lanes = onehot(iota((128, points), 0) == lane)
    high, low = two_parts(adjoint)
    parts = jnp.concatenate([high.astype(BF16), low.astype(BF16)], axis=1)
    picked = jnp.dot(
        parts, jnp.concatenate([lanes, lanes], axis=0), preferred_element_type=F32
    )
    row_mask = iota((64, points), 0) == row
    scale = jnp.where(live, weight, 0.0)
    words = [
        jnp.sum(
            jnp.where(row_mask, picked[64 * f : 64 * f + 64], 0.0),
            axis=0,
            keepdims=True,
        )
        * scale
        for f in range(5)
    ]
    words.append(target.astype(F32))
    place = (dest & 96) | ((dest & 3) << 3) | ((dest >> 2) & 7)
    place = jnp.where(live, place, -1)
    tiles = jnp.where(iota((128, points), 0) == place, 1.0, 0.0)
    tiles16 = tiles.astype(BF16)
    before = onehot(iota((256, 256), 0) < iota((256, 256), 1))
    ranks = []
    earlier = jnp.zeros((128, 1), F32)
    for b in range(points // 256):
        block = tiles[:, 256 * b : 256 * b + 256]
        counts = jnp.dot(
            tiles16[:, 256 * b : 256 * b + 256], before, preferred_element_type=F32
        )
        ranks.append(jnp.sum(block * (counts + earlier), axis=0, keepdims=True))
        earlier = earlier + jnp.sum(block, axis=1, keepdims=True)
    rank = jnp.concatenate(ranks, axis=1).astype(jnp.int32)
    eight = iota((8, points), 0)
    first, second, third = eight == rank, eight + 8 == rank, (eight & 3) + 16 == rank
    halves = [two_parts(w) for w in words]
    sides = []
    for side in (0, 1):
        groups = []
        for a, b in ((0, 1), (2, 3), (4, 5)):
            one, two = halves[a][side], halves[b][side]
            groups += [
                jnp.where(first, one, 0.0),
                jnp.where(second, one, 0.0),
                jnp.where(third, jnp.where(eight < 4, one, two), 0.0),
                jnp.where(first, two, 0.0),
                jnp.where(second, two, 0.0),
            ]
        groups.append(jnp.zeros((8, points), F32))
        sides.append(jnp.concatenate(groups, axis=0).astype(BF16))
    packed = lax.dot_general(
        tiles16,
        jnp.concatenate(sides, axis=0),
        (((1,), (1,)), ((), ())),
        preferred_element_type=F32,
    )
    return packed[:, :128] + packed[:, 128:]


def spread(block_ref, lhs_ref, rhs_ref):
    row_iota, lane_iota = iota((32, 128), 0), iota((256, 128), 0)
    for slot in range(SLOTS):
        where = word_row(5, slot)
        target = block_ref[where : where + 1, :].astype(jnp.int32)
        row = (target >> 7) & 31
        lane = (target & 127) | ((target >> 12) << 7)
        row_mask = row_iota == row
        columns = slice(128 * slot, 128 * slot + 128)
        rhs_ref[:, columns] = onehot(lane_iota == lane)
        for f in range(5):
            at = word_row(f, slot)
            high, low = two_parts(block_ref[at : at + 1, :])
            lhs_ref[32 * f : 32 * f + 32, columns] = jnp.where(
                row_mask, high, 0.0
            ).astype(BF16)
            lhs_ref[160 + 32 * f : 192 + 32 * f, columns] = jnp.where(
                row_mask, low, 0.0
            ).astype(BF16)


def differences(at):
    return (
        45.0 * (at(1) - at(-1)) - 9.0 * (at(2) - at(-2)) + (at(3) - at(-3))
    ) * (1.0 / 60.0)


def kernel(
    adjoint_hbm,
    flow_hbm,
    cell_hbm,
    dest_hbm,
    target_hbm,
    weight_hbm,
    count_hbm,
    out_ref,
    adjoint_ref,
    flow_ref,
    cell_ref,
    dest_ref,
    target_ref,
    weight_ref,
    count_ref,
    packed_ref,
    plane_ref,
    column_ref,
    near_ref,
    turned_ref,
    lhs_ref,
    rhs_ref,
    x_ref,
    y_ref,
    swap_ref,
    in_sem,
    turn_sem,
    close_sem,
    wide_sem,
    plane_send,
    plane_recv,
    near_send,
    near_recv,
    halo_send,
    halo_recv,
):
    loads = [
        pltpu.make_async_copy(src, dst, in_sem.at[i])
        for i, (src, dst) in enumerate(
            (
                (adjoint_hbm, adjoint_ref),
                (flow_hbm, flow_ref),
                (cell_hbm, cell_ref),
                (dest_hbm, dest_ref),
                (target_hbm, target_ref),
                (weight_hbm, weight_ref),
                (count_hbm, count_ref),
            )
        )
    ]
    for load in loads:
        load.start()

    sec, gx, gy = lax.axis_index("sec"), lax.axis_index("gx"), lax.axis_index("gy")
    n_gx, n_gy = lax.axis_size("gx"), lax.axis_size("gy")
    y, z = gx // NZ_DEV, gx % NZ_DEV
    is_far = sec < FAR
    is_near = sec == FAR
    core = sec % 2
    first_core = sec - core
    low_half = sec < 2
    me = y * NX_DEV + gy
    last_z = z == NZ_DEV - 1
    high_turn, low_turn = (gx < n_gx - 1) & last_z, (gx > 0) & (z == 0)

    barrier = pltpu.get_barrier_semaphore()

    def tell(condition, device):
        @pl.when(condition)
        def _():
            pl.semaphore_signal(barrier, inc=1, device_id=device)

    one, zero = jnp.int32(1), jnp.int32(0)

    def number(condition):
        return jnp.where(condition, one, zero)

    has_low, has_high = gx > 0, gx < n_gx - 1
    neighbours = (
        (has_low, {"gx": gx - 1}),
        (has_high, {"gx": gx + 1}),
        (gy > 0, {"gy": gy - 1}),
        (gy < n_gy - 1, {"gy": gy + 1}),
    )
    tell(has_low & (z > 0), {"sec": first_core, "gx": gx - 1})
    tell(low_turn, {"sec": first_core + 1, "gx": gx - 1})
    tell(has_high & jnp.logical_not(last_z), {"sec": first_core, "gx": gx + 1})
    tell(high_turn, {"sec": first_core + 1, "gx": gx + 1})
    tell(gy > 0, {"sec": first_core, "gy": gy - 1})
    tell(gy < n_gy - 1, {"sec": first_core, "gy": gy + 1})
    tell(core == 1, {"sec": first_core})
    tell(core == 0, {"sec": first_core + 1})
    tell(last_z, {"sec": first_core + 1, "gx": gx - 1})

    def plane_peer(step):
        q = (me + step) % PLANE
        return q, {"gx": (q // NX_DEV) * NZ_DEV + z, "gy": q % NX_DEV}

    @pl.when(is_far)
    def _():
        @pl.loop(1, PLANE)
        def _(step):
            to = {"sec": first_core, **plane_peer(step)[1]}
            pl.semaphore_signal(barrier, inc=1, device_id=to)

    @pl.when(is_near)
    def _():
        @pl.loop(0, NZ_DEV - 1)
        def _(i):
            to = {"sec": 1, "gx": y * NZ_DEV + i}
            pl.semaphore_signal(barrier, inc=1, device_id=to)

        @pl.loop(0, NZ_DEV - 1)
        def _(i):
            @pl.when(i != z)
            def _():
                to = {"gx": y * NZ_DEV + i}
                pl.semaphore_signal(barrier, inc=1, device_id=to)

    close_count = (
        2
        * (
            number(has_low & (z > 0))
            + number(has_high & jnp.logical_not(last_z))
            + number(gy > 0)
            + number(gy < n_gy - 1)
        )
        + (PLANE - 1) * jnp.where(low_half, 2, 1)
        + 1
    )
    wide_count = (
        jnp.where(low_half, NZ_DEV, NZ_DEV - 1)
        + 2 * number(low_turn)
        + 2 * number(z == NZ_DEV - 2)
        + 1
    )
    turn_count = 2 * number(high_turn) + 1

    loads[0].wait()
    loads[1].wait()

    a = [adjoint_ref[64 * f : 64 * f + 64, :] for f in range(5)]
    density, m1, m2, m3, energy, sponge = (
        flow_ref[64 * f : 64 * f + 64, :] for f in range(6)
    )
    inverse = 1.0 / density
    velocity = [m * inverse for m in (m1, m2, m3)]
    kinetic = 0.5 * (m1 * m1 + m2 * m2 + m3 * m3) * inverse
    stiffness = GAMMA_RATIO * (GAMMA_MINUS * (energy - kinetic))
    pressure_like = density * a[0] + stiffness * a[4]

    def flux(direction):
        f = [velocity[direction] * a[i] for i in range(5)]
        f[1 + direction] = f[1 + direction] + pressure_like
        f[4] = f[4] + a[1 + direction] * inverse
        return f

    for f, value in enumerate(flux(0)):
        x_ref[f, 3:11] = value.reshape(8, 8, 128)
    halos = []
    for ref, low, high in ((x_ref, 0, 1), (y_ref, 2, 3)):
        halos.append((ref, low, 3, 11, high))
        halos.append((ref, high, 8, 0, low))

    def halo_copy(i):
        ref, side, first, there, _ = halos[i]
        return pltpu.make_async_remote_copy(
            src_ref=ref.at[:, pl.ds(first, 3)],
            dst_ref=ref.at[:, pl.ds(there, 3)],
            send_sem=halo_send.at[i],
            recv_sem=halo_recv.at[i],
            device_id=neighbours[side][1],
        )

    @pl.when(last_z & (core == 1))
    def _():
        pl.semaphore_wait(barrier, turn_count)
        pl.semaphore_signal(turn_sem, inc=1, device_id={"sec": first_core})

    @pl.when(last_z & (core == 0))
    def _():
        pl.semaphore_wait(turn_sem, 1)

    @pl.when(high_turn)
    def _():
        halo_copy(1).start()

    for load in loads[2:]:
        load.wait()

    @pl.when(is_far)
    def _():
        packed_ref[...] = pack(
            adjoint_ref[...],
            cell_ref[...],
            dest_ref[...],
            target_ref[...],
            weight_ref[...],
            count_ref[0, 0, 0],
        )

    for f, value in enumerate(flux(1)):
        swap_ref[64 * f : 64 * f + 64, :] = value
    for f in range(5):
        for j in range(8):
            y_ref[f, 3 + j] = swap_ref[pl.ds(64 * f + j, 8, stride=8), :]

    @pl.when(core == 0)
    def _():
        pl.semaphore_wait(barrier, close_count)
        pl.semaphore_signal(close_sem, inc=1, device_id={"sec": first_core + 1})

    @pl.when(core == 1)
    def _():
        pl.semaphore_wait(close_sem, 1)

    def own_copy():
        return pltpu.make_async_copy(
            packed_ref.at[pl.ds(pl.multiple_of(me * 8, 8), 8)],
            plane_ref.at[me],
            plane_recv,
        )

    def plane_copy(step):
        q, device = plane_peer(step)
        return pltpu.make_async_remote_copy(
            src_ref=packed_ref.at[pl.ds(pl.multiple_of(q * 8, 8), 8)],
            dst_ref=plane_ref.at[me],
            send_sem=plane_send,
            recv_sem=plane_recv,
            device_id=device,
        )

    chunk = jnp.where(low_half, 1 + z // 4, 0)
    place = jnp.where(low_half, 4 * core + z % 4, z)

    def near_copy(step):
        z_to = (z + step) % NZ_DEV
        return pltpu.make_async_remote_copy(
            src_ref=column_ref.at[z_to],
            dst_ref=near_ref.at[chunk, place],
            send_sem=near_send,
            recv_sem=near_recv.at[chunk],
            device_id={"sec": FAR, "gx": y * NZ_DEV + z_to},
        )

    @pl.when(is_far)
    def _():
        own_copy().start()

        @pl.loop(1, PLANE)
        def _(step):
            plane_copy(step).start()

    for i in (1, 0, 2, 3):
        ref, side, _, there, other = halos[i]
        now = neighbours[side][0]
        if i == 0:
            now = now & (z > 0)
        if i == 1:
            now = now & jnp.logical_not(last_z)

        @pl.when(now)
        def _(i=i):
            halo_copy(i).start()

        @pl.when(jnp.logical_not(neighbours[other][0]))
        def _(ref=ref, there=there):
            ref[:, there : there + 3] = jnp.zeros((5, 3, 8, 128), F32)

    flux_z = flux(2)
    for f in range(5):
        value = flux_z[f]
        along_z = differences(lambda o: pltpu.roll(value, (-o) % 128, 1))
        out_ref[64 * f : 64 * f + 64, :] = a[f] + STEP_SIZE * (along_z - sponge * a[f])

    def add_x(first, last):
        rows = 8 * (last - first)
        for f in range(5):
            along_x = differences(lambda o: x_ref[f, 3 + first + o : 3 + last + o])
            at = 64 * f + 8 * first
            out_ref[at : at + rows, :] += STEP_SIZE * along_x.reshape(rows, 128)

    add_x(3, 5)

    @pl.when(is_far)
    def _():
        pltpu.make_async_copy(plane_ref, plane_ref, plane_recv).wait()
        for to in range(NZ_DEV):
            column_ref[to] = plane_ref[:, to, :]

    @pl.when((core == 1) & jnp.logical_not(last_z))
    def _():
        pl.semaphore_wait(barrier, wide_count)
        pl.semaphore_signal(wide_sem, inc=1, device_id={"sec": first_core})

        @pl.when(z == NZ_DEV - 2)
        def _():
            for to in (0, 1):
                device = {"sec": first_core + to, "gx": gx + 1}
                pl.semaphore_signal(wide_sem, inc=1, device_id=device)

    @pl.when((core == 0) | last_z)
    def _():
        pl.semaphore_wait(wide_sem, 1)

    @pl.when(low_turn)
    def _():
        halo_copy(0).start()

    @pl.when(is_far)
    def _():
        @pl.loop(0, NZ_DEV)
        def _(step):
            near_copy(step).start()

    def receive(i):
        @pl.when(neighbours[halos[i][4]][0])
        def _():
            halo_copy(i).wait_recv()

    receive(2)
    receive(3)
    for f in range(5):
        along_y = differences(lambda o: y_ref[f, 3 + o : 11 + o])
        swap_ref[64 * f : 64 * f + 64, :] = along_y.reshape(64, 128)
    for f in range(5):
        for j in range(8):
            at = 64 * f + 8 * j
            out_ref[at : at + 8, :] += (
                STEP_SIZE * swap_ref[pl.ds(64 * f + j, 8, stride=8), :]
            )
    receive(0)
    add_x(5, 8)
    receive(1)
    add_x(0, 3)

    @pl.when(is_near)
    def _():
        @pl.loop(0, FAR)
        def _(i):
            pltpu.make_async_copy(
                near_ref.at[i], near_ref.at[i], near_recv.at[i]
            ).wait()
            turned_ref[...] = near_ref[i].reshape(128, 128).T
            spread(turned_ref, lhs_ref, rhs_ref)
            total = lax.dot_general(
                lhs_ref[...],
                rhs_ref[...],
                (((1,), (1,)), ((), ())),
                preferred_element_type=F32,
            )
            total = STEP_SIZE * (total[:160] + total[160:])
            for f in range(5):
                part = total[32 * f : 32 * f + 32]
                out_ref[64 * f : 64 * f + 32, :] += part[:, :128]
                out_ref[64 * f + 32 : 64 * f + 64, :] += part[:, 128:]

    for i in range(4):

        @pl.when(neighbours[halos[i][1]][0])
        def _(i=i):
            halo_copy(i).wait_send()

    @pl.when(is_far)
    def _():
        others = packed_ref.at[pl.ds(0, 8 * (PLANE - 1))]
        pltpu.make_async_copy(others, others, plane_send).wait()
        pltpu.make_async_copy(column_ref, column_ref, near_send).wait()


def local(adjoint, flow, point_cell, point_dest, point_target, point_weight, point_count):
    points = point_cell.shape[-1]
    hbm = pl.BlockSpec(memory_space=pl.ANY)
    out = pl.pallas_call(
        kernel,
        out_shape=jax.ShapeDtypeStruct((320, 128), F32),
        in_specs=[hbm] * 7,
        out_specs=pl.BlockSpec(memory_space=pltpu.VMEM),
        scratch_shapes=[
            pltpu.VMEM((320, 128), F32),
            pltpu.VMEM((384, 128), F32),
            pltpu.VMEM((1, points), jnp.int32),
            pltpu.VMEM((1, points), jnp.int32),
            pltpu.VMEM((1, points), jnp.int32),
            pltpu.VMEM((1, points), F32),
            pltpu.SMEM((1, 1, 1), jnp.int32),
            pltpu.VMEM((128, 128), F32),
            pltpu.VMEM((PLANE, NZ_DEV, 128), F32),
            pltpu.VMEM((NZ_DEV, PLANE, 128), F32),
            pltpu.VMEM((FAR, NZ_DEV, PLANE, 128), F32),
            pltpu.VMEM((128, 128), F32),
            pltpu.VMEM((320, SLOTS * 128), BF16),
            pltpu.VMEM((256, SLOTS * 128), BF16),
            pltpu.VMEM((5, 14, 8, 128), F32),
            pltpu.VMEM((5, 14, 8, 128), F32),
            pltpu.VMEM((320, 128), F32),
            pltpu.SemaphoreType.DMA((7,)),
            pltpu.SemaphoreType.REGULAR,
            pltpu.SemaphoreType.REGULAR,
            pltpu.SemaphoreType.REGULAR,
            pltpu.SemaphoreType.DMA,
            pltpu.SemaphoreType.DMA,
            pltpu.SemaphoreType.DMA,
            pltpu.SemaphoreType.DMA((FAR,)),
            pltpu.SemaphoreType.DMA((4,)),
            pltpu.SemaphoreType.DMA((4,)),
        ],
        cost_estimate=pl.CostEstimate(
            flops=2 * 10**9, bytes_accessed=10**6, transcendentals=0
        ),
        compiler_params=pltpu.CompilerParams(
            collective_id=0, has_side_effects=True, vmem_limit_bytes=VMEM_BYTES
        ),
    )(
        *(
            pltpu.with_memory_space_constraint(v, pltpu.HBM)
            for v in (
                adjoint.reshape(320, 128),
                flow.reshape(384, 128),
                point_cell.reshape(1, points),
                point_dest.reshape(1, points),
                point_target.reshape(1, points),
                point_weight.reshape(1, points),
            )
        ),
        point_count,
    )
    return out.reshape(1, 5, 8, 8, 128)


def solution(mesh):
    placed = (
        P("sec", None, "gx", "gy", None),
        P("sec", None, "gx", "gy", None),
        P("sec", "gx", "gy", None),
        P("sec", "gx", "gy", None),
        P("sec", "gx", "gy", None),
        P("sec", "gx", "gy", None),
        P("sec", "gx", "gy"),
    )
    return jax.shard_map(
        local,
        mesh=mesh,
        in_specs=placed,
        out_specs=P("sec", None, "gx", "gy", None),
        check_vma=False,
    )
```

```python
import jax
import jax.numpy as jnp
from jax import lax
from jax.experimental import pallas as pl
from jax.experimental.pallas import tpu as pltpu
from jax.sharding import PartitionSpec as P

GAMMA_MINUS = 0.4
GAMMA_RATIO = 1.4
STEP_SIZE = 0.4
FAR = 3
NZ_DEV = 8
NY_DEV = 4
NX_DEV = 4
PLANE = NY_DEV * NX_DEV
STEPS = sorted(
    ((i, j) for i in range(NY_DEV) for j in range(NX_DEV) if i or j),
    key=lambda s: -min(s[0], NY_DEV - s[0]) - min(s[1], NX_DEV - s[1]),
)
SLOTS = 20
VMEM_BYTES = 40 * 1024 * 1024
F32 = jnp.float32
BF16 = jnp.bfloat16


def iota(shape, dim):
    return lax.broadcasted_iota(jnp.int32, shape, dim)


def two_parts(x):
    high = x.astype(BF16).astype(F32)
    return high, (x - high).astype(BF16).astype(F32)


def onehot(condition):
    return jnp.where(condition, 1.0, 0.0).astype(BF16)


def word_row(word, slot):
    base = 40 * (word // 2)
    return base + slot if word % 2 == 0 else base + 20 + (slot + 4) % 20


def pack(adjoint, cell, dest, target, weight, count):
    points = cell.shape[1]
    live = iota((1, points), 1) < count
    row, lane = cell >> 7, cell & 127
    lanes = onehot(iota((128, points), 0) == lane)
    high, low = two_parts(adjoint)
    parts = jnp.concatenate([high.astype(BF16), low.astype(BF16)], axis=1)
    picked = jnp.dot(
        parts, jnp.concatenate([lanes, lanes], axis=0), preferred_element_type=F32
    )
    row_mask = iota((64, points), 0) == row
    scale = jnp.where(live, weight, 0.0)
    words = [
        jnp.sum(
            jnp.where(row_mask, picked[64 * f : 64 * f + 64], 0.0),
            axis=0,
            keepdims=True,
        )
        * scale
        for f in range(5)
    ]
    words.append(target.astype(F32))
    place = (dest & 96) | ((dest & 3) << 3) | ((dest >> 2) & 7)
    place = jnp.where(live, place, -1)
    tiles = jnp.where(iota((128, points), 0) == place, 1.0, 0.0)
    tiles16 = tiles.astype(BF16)
    before = onehot(iota((256, 256), 0) < iota((256, 256), 1))
    ranks = []
    earlier = jnp.zeros((128, 1), F32)
    for b in range(points // 256):
        block = tiles[:, 256 * b : 256 * b + 256]
        counts = jnp.dot(
            tiles16[:, 256 * b : 256 * b + 256], before, preferred_element_type=F32
        )
        ranks.append(jnp.sum(block * (counts + earlier), axis=0, keepdims=True))
        earlier = earlier + jnp.sum(block, axis=1, keepdims=True)
    rank = jnp.concatenate(ranks, axis=1).astype(jnp.int32)
    eight = iota((8, points), 0)
    first, second, third = eight == rank, eight + 8 == rank, (eight & 3) + 16 == rank
    halves = [two_parts(w) for w in words]
    sides = []
    for side in (0, 1):
        groups = []
        for a, b in ((0, 1), (2, 3), (4, 5)):
            one, two = halves[a][side], halves[b][side]
            groups += [
                jnp.where(first, one, 0.0),
                jnp.where(second, one, 0.0),
                jnp.where(third, jnp.where(eight < 4, one, two), 0.0),
                jnp.where(first, two, 0.0),
                jnp.where(second, two, 0.0),
            ]
        groups.append(jnp.zeros((8, points), F32))
        sides.append(jnp.concatenate(groups, axis=0).astype(BF16))
    packed = lax.dot_general(
        tiles16,
        jnp.concatenate(sides, axis=0),
        (((1,), (1,)), ((), ())),
        preferred_element_type=F32,
    )
    return packed[:, :128] + packed[:, 128:]


def spread(block_ref, lhs_ref, rhs_ref):
    row_iota, lane_iota = iota((32, 128), 0), iota((256, 128), 0)
    for slot in range(SLOTS):
        where = word_row(5, slot)
        target = block_ref[where : where + 1, :].astype(jnp.int32)
        row = (target >> 7) & 31
        lane = (target & 127) | ((target >> 12) << 7)
        row_mask = row_iota == row
        columns = slice(128 * slot, 128 * slot + 128)
        rhs_ref[:, columns] = onehot(lane_iota == lane)
        for f in range(5):
            at = word_row(f, slot)
            high, low = two_parts(block_ref[at : at + 1, :])
            lhs_ref[32 * f : 32 * f + 32, columns] = jnp.where(
                row_mask, high, 0.0
            ).astype(BF16)
            lhs_ref[160 + 32 * f : 192 + 32 * f, columns] = jnp.where(
                row_mask, low, 0.0
            ).astype(BF16)


def differences(at):
    return (
        45.0 * (at(1) - at(-1)) - 9.0 * (at(2) - at(-2)) + (at(3) - at(-3))
    ) * (1.0 / 60.0)


def kernel(
    adjoint_hbm,
    flow_hbm,
    cell_hbm,
    dest_hbm,
    target_hbm,
    weight_hbm,
    count_hbm,
    out_ref,
    adjoint_ref,
    flow_ref,
    cell_ref,
    dest_ref,
    target_ref,
    weight_ref,
    count_ref,
    packed_ref,
    plane_ref,
    column_ref,
    near_ref,
    turned_ref,
    lhs_ref,
    rhs_ref,
    x_ref,
    y_ref,
    swap_ref,
    in_sem,
    turn_sem,
    close_sem,
    wide_sem,
    plane_send,
    plane_recv,
    near_send,
    near_recv,
    halo_send,
    halo_recv,
):
    loads = [
        pltpu.make_async_copy(src, dst, in_sem.at[i])
        for i, (src, dst) in enumerate(
            (
                (adjoint_hbm, adjoint_ref),
                (flow_hbm, flow_ref),
                (cell_hbm, cell_ref),
                (dest_hbm, dest_ref),
                (target_hbm, target_ref),
                (weight_hbm, weight_ref),
                (count_hbm, count_ref),
            )
        )
    ]
    for load in loads:
        load.start()

    sec, gx, gy = lax.axis_index("sec"), lax.axis_index("gx"), lax.axis_index("gy")
    n_gx, n_gy = lax.axis_size("gx"), lax.axis_size("gy")
    y, z = gx // NZ_DEV, gx % NZ_DEV
    is_far = sec < FAR
    is_near = sec == FAR
    core = sec % 2
    first_core = sec - core
    low_half = sec < 2
    me = y * NX_DEV + gy
    last_z = z == NZ_DEV - 1
    high_turn, low_turn = (gx < n_gx - 1) & last_z, (gx > 0) & (z == 0)

    barrier = pltpu.get_barrier_semaphore()

    def tell(condition, device):
        @pl.when(condition)
        def _():
            pl.semaphore_signal(barrier, inc=1, device_id=device)

    one, zero = jnp.int32(1), jnp.int32(0)

    def number(condition):
        return jnp.where(condition, one, zero)

    has_low, has_high = gx > 0, gx < n_gx - 1
    neighbours = (
        (has_low, {"gx": gx - 1}),
        (has_high, {"gx": gx + 1}),
        (gy > 0, {"gy": gy - 1}),
        (gy < n_gy - 1, {"gy": gy + 1}),
    )
    def plane_peer(step):
        to_y, to_x = (y + step[0]) % NY_DEV, (gy + step[1]) % NX_DEV
        return to_y * NX_DEV + to_x, {"gx": to_y * NZ_DEV + z, "gy": to_x}

    @pl.when(is_near)
    def _():
        @pl.loop(0, NZ_DEV)
        def _(i):
            z_to = (z + i) % NZ_DEV

            @pl.when(z_to < NZ_DEV - 1)
            def _():
                to = {"sec": 1, "gx": y * NZ_DEV + z_to}
                pl.semaphore_signal(barrier, inc=1, device_id=to)

        @pl.loop(0, NZ_DEV - 1)
        def _(i):
            @pl.when(i != z)
            def _():
                to = {"gx": y * NZ_DEV + i}
                pl.semaphore_signal(barrier, inc=1, device_id=to)

    @pl.when(is_far)
    def _():
        for step in STEPS:
            to = {"sec": first_core, **plane_peer(step)[1]}
            pl.semaphore_signal(barrier, inc=1, device_id=to)

    tell(has_low & (z > 0), {"sec": first_core, "gx": gx - 1})
    tell(low_turn, {"sec": first_core + 1, "gx": gx - 1})
    tell(has_high & jnp.logical_not(last_z), {"sec": first_core, "gx": gx + 1})
    tell(high_turn, {"sec": first_core + 1, "gx": gx + 1})
    tell(gy > 0, {"sec": first_core, "gy": gy - 1})
    tell(gy < n_gy - 1, {"sec": first_core, "gy": gy + 1})
    tell(core == 1, {"sec": first_core})
    tell(core == 0, {"sec": first_core + 1})
    tell(last_z, {"sec": first_core + 1, "gx": gx - 1})

    close_count = (
        2
        * (
            number(has_low & (z > 0))
            + number(has_high & jnp.logical_not(last_z))
            + number(gy > 0)
            + number(gy < n_gy - 1)
        )
        + (PLANE - 1) * jnp.where(low_half, 2, 1)
        + 1
    )
    wide_count = (
        jnp.where(low_half, NZ_DEV, NZ_DEV - 1)
        + 2 * number(low_turn)
        + 2 * number(z == NZ_DEV - 2)
        + 1
    )
    turn_count = 2 * number(high_turn) + 1

    loads[0].wait()
    loads[1].wait()

    a = [adjoint_ref[64 * f : 64 * f + 64, :] for f in range(5)]
    density, m1, m2, m3, energy, sponge = (
        flow_ref[64 * f : 64 * f + 64, :] for f in range(6)
    )
    inverse = 1.0 / density
    velocity = [m * inverse for m in (m1, m2, m3)]
    kinetic = 0.5 * (m1 * m1 + m2 * m2 + m3 * m3) * inverse
    stiffness = GAMMA_RATIO * (GAMMA_MINUS * (energy - kinetic))
    pressure_like = density * a[0] + stiffness * a[4]

    def flux(direction):
        f = [velocity[direction] * a[i] for i in range(5)]
        f[1 + direction] = f[1 + direction] + pressure_like
        f[4] = f[4] + a[1 + direction] * inverse
        return f

    for f, value in enumerate(flux(0)):
        x_ref[f, 3:11] = value.reshape(8, 8, 128)
    halos = []
    for ref, low, high in ((x_ref, 0, 1), (y_ref, 2, 3)):
        halos.append((ref, low, 3, 11, high))
        halos.append((ref, high, 8, 0, low))

    def halo_copy(i):
        ref, side, first, there, _ = halos[i]
        return pltpu.make_async_remote_copy(
            src_ref=ref.at[:, pl.ds(first, 3)],
            dst_ref=ref.at[:, pl.ds(there, 3)],
            send_sem=halo_send.at[i],
            recv_sem=halo_recv.at[i],
            device_id=neighbours[side][1],
        )

    @pl.when(last_z & (core == 1))
    def _():
        pl.semaphore_wait(barrier, turn_count)
        pl.semaphore_signal(turn_sem, inc=1, device_id={"sec": first_core})

    @pl.when(last_z & (core == 0))
    def _():
        pl.semaphore_wait(turn_sem, 1)

    @pl.when(high_turn)
    def _():
        halo_copy(1).start()

    for load in loads[2:]:
        load.wait()

    @pl.when(is_far)
    def _():
        packed_ref[...] = pack(
            adjoint_ref[...],
            cell_ref[...],
            dest_ref[...],
            target_ref[...],
            weight_ref[...],
            count_ref[0, 0, 0],
        )

    for f, value in enumerate(flux(1)):
        swap_ref[64 * f : 64 * f + 64, :] = value
    for f in range(5):
        for j in range(8):
            y_ref[f, 3 + j] = swap_ref[pl.ds(64 * f + j, 8, stride=8), :]

    @pl.when(core == 0)
    def _():
        pl.semaphore_wait(barrier, close_count)
        pl.semaphore_signal(close_sem, inc=1, device_id={"sec": first_core + 1})

    @pl.when(core == 1)
    def _():
        pl.semaphore_wait(close_sem, 1)

    def own_copy():
        return pltpu.make_async_copy(
            packed_ref.at[pl.ds(pl.multiple_of(me * 8, 8), 8)],
            plane_ref.at[me],
            plane_recv,
        )

    def plane_copy(step):
        q, device = plane_peer(step)
        return pltpu.make_async_remote_copy(
            src_ref=packed_ref.at[pl.ds(pl.multiple_of(q * 8, 8), 8)],
            dst_ref=plane_ref.at[me],
            send_sem=plane_send,
            recv_sem=plane_recv,
            device_id=device,
        )

    chunk = jnp.where(low_half, 1 + z // 4, 0)
    place = jnp.where(low_half, 4 * core + z % 4, z)

    def near_copy(step):
        low_to = jnp.where(z < 4, z + step, z - step + NZ_DEV) % NZ_DEV
        high_to = jnp.where(z < 4, NZ_DEV - 1 - step, step)
        z_to = jnp.where(low_half, low_to, high_to)
        return pltpu.make_async_remote_copy(
            src_ref=column_ref.at[z_to],
            dst_ref=near_ref.at[chunk, place],
            send_sem=near_send,
            recv_sem=near_recv.at[chunk],
            device_id={"sec": FAR, "gx": y * NZ_DEV + z_to},
        )

    @pl.when(is_far)
    def _():
        own_copy().start()

        for step in STEPS:
            plane_copy(step).start()

        def _(step):
            plane_copy(step).start()

    def start_halo(i, condition):
        @pl.when(neighbours[halos[i][1]][0] & condition)
        def _():
            halo_copy(i).start()

    start_halo(1, jnp.logical_not(last_z))
    start_halo(0, z > 0)
    start_halo(2, is_near)
    start_halo(3, is_near)
    for ref, _, _, there, other in halos:

        @pl.when(jnp.logical_not(neighbours[other][0]))
        def _(ref=ref, there=there):
            ref[:, there : there + 3] = jnp.zeros((5, 3, 8, 128), F32)

    flux_z = flux(2)
    for f in range(5):
        value = flux_z[f]
        along_z = differences(lambda o: pltpu.roll(value, (-o) % 128, 1))
        out_ref[64 * f : 64 * f + 64, :] = a[f] + STEP_SIZE * (along_z - sponge * a[f])

    def add_x(first, last):
        rows = 8 * (last - first)
        for f in range(5):
            along_x = differences(lambda o: x_ref[f, 3 + first + o : 3 + last + o])
            at = 64 * f + 8 * first
            out_ref[at : at + rows, :] += STEP_SIZE * along_x.reshape(rows, 128)

    add_x(3, 5)

    @pl.when(is_far)
    def _():
        pltpu.make_async_copy(plane_ref, plane_ref, plane_recv).wait()
        for to in range(NZ_DEV):
            column_ref[to] = plane_ref[:, to, :]

    start_halo(2, is_far)
    start_halo(3, is_far)

    @pl.when((core == 1) & jnp.logical_not(last_z))
    def _():
        pl.semaphore_wait(barrier, wide_count)
        pl.semaphore_signal(wide_sem, inc=1, device_id={"sec": first_core})

        @pl.when(z == NZ_DEV - 2)
        def _():
            for to in (0, 1):
                device = {"sec": first_core + to, "gx": gx + 1}
                pl.semaphore_signal(wide_sem, inc=1, device_id=device)

    @pl.when((core == 0) | last_z)
    def _():
        pl.semaphore_wait(wide_sem, 1)

    @pl.when(low_turn)
    def _():
        halo_copy(0).start()

    @pl.when(is_far)
    def _():
        @pl.loop(0, NZ_DEV)
        def _(step):
            near_copy(step).start()

    def receive(i):
        @pl.when(neighbours[halos[i][4]][0])
        def _():
            halo_copy(i).wait_recv()

    receive(2)
    receive(3)
    for f in range(5):
        along_y = differences(lambda o: y_ref[f, 3 + o : 11 + o])
        swap_ref[64 * f : 64 * f + 64, :] = along_y.reshape(64, 128)
    for f in range(5):
        for j in range(8):
            at = 64 * f + 8 * j
            out_ref[at : at + 8, :] += (
                STEP_SIZE * swap_ref[pl.ds(64 * f + j, 8, stride=8), :]
            )
    receive(0)
    add_x(5, 8)
    receive(1)
    add_x(0, 3)

    @pl.when(is_near)
    def _():
        @pl.loop(0, FAR)
        def _(i):
            k = lax.rem(i + 1, FAR)
            pltpu.make_async_copy(
                near_ref.at[k], near_ref.at[k], near_recv.at[k]
            ).wait()
            turned_ref[...] = near_ref[k].reshape(128, 128).T
            spread(turned_ref, lhs_ref, rhs_ref)
            total = lax.dot_general(
                lhs_ref[...],
                rhs_ref[...],
                (((1,), (1,)), ((), ())),
                preferred_element_type=F32,
            )
            total = STEP_SIZE * (total[:160] + total[160:])
            for f in range(5):
                part = total[32 * f : 32 * f + 32]
                out_ref[64 * f : 64 * f + 32, :] += part[:, :128]
                out_ref[64 * f + 32 : 64 * f + 64, :] += part[:, 128:]

    for i in range(4):

        @pl.when(neighbours[halos[i][1]][0])
        def _(i=i):
            halo_copy(i).wait_send()

    @pl.when(is_far)
    def _():
        others = packed_ref.at[pl.ds(0, 8 * (PLANE - 1))]
        pltpu.make_async_copy(others, others, plane_send).wait()
        pltpu.make_async_copy(column_ref, column_ref, near_send).wait()


def local(adjoint, flow, point_cell, point_dest, point_target, point_weight, point_count):
    points = point_cell.shape[-1]
    hbm = pl.BlockSpec(memory_space=pl.ANY)
    out = pl.pallas_call(
        kernel,
        out_shape=jax.ShapeDtypeStruct((320, 128), F32),
        in_specs=[hbm] * 7,
        out_specs=pl.BlockSpec(memory_space=pltpu.VMEM),
        scratch_shapes=[
            pltpu.VMEM((320, 128), F32),
            pltpu.VMEM((384, 128), F32),
            pltpu.VMEM((1, points), jnp.int32),
            pltpu.VMEM((1, points), jnp.int32),
            pltpu.VMEM((1, points), jnp.int32),
            pltpu.VMEM((1, points), F32),
            pltpu.SMEM((1, 1, 1), jnp.int32),
            pltpu.VMEM((128, 128), F32),
            pltpu.VMEM((PLANE, NZ_DEV, 128), F32),
            pltpu.VMEM((NZ_DEV, PLANE, 128), F32),
            pltpu.VMEM((FAR, NZ_DEV, PLANE, 128), F32),
            pltpu.VMEM((128, 128), F32),
            pltpu.VMEM((320, SLOTS * 128), BF16),
            pltpu.VMEM((256, SLOTS * 128), BF16),
            pltpu.VMEM((5, 14, 8, 128), F32),
            pltpu.VMEM((5, 14, 8, 128), F32),
            pltpu.VMEM((320, 128), F32),
            pltpu.SemaphoreType.DMA((7,)),
            pltpu.SemaphoreType.REGULAR,
            pltpu.SemaphoreType.REGULAR,
            pltpu.SemaphoreType.REGULAR,
            pltpu.SemaphoreType.DMA,
            pltpu.SemaphoreType.DMA,
            pltpu.SemaphoreType.DMA,
            pltpu.SemaphoreType.DMA((FAR,)),
            pltpu.SemaphoreType.DMA((4,)),
            pltpu.SemaphoreType.DMA((4,)),
        ],
        cost_estimate=pl.CostEstimate(
            flops=2 * 10**9, bytes_accessed=10**6, transcendentals=0
        ),
        compiler_params=pltpu.CompilerParams(
            collective_id=0, has_side_effects=True, vmem_limit_bytes=VMEM_BYTES
        ),
    )(
        *(
            pltpu.with_memory_space_constraint(v, pltpu.HBM)
            for v in (
                adjoint.reshape(320, 128),
                flow.reshape(384, 128),
                point_cell.reshape(1, points),
                point_dest.reshape(1, points),
                point_target.reshape(1, points),
                point_weight.reshape(1, points),
            )
        ),
        point_count,
    )
    return out.reshape(1, 5, 8, 8, 128)


def solution(mesh):
    placed = (
        P("sec", None, "gx", "gy", None),
        P("sec", None, "gx", "gy", None),
        P("sec", "gx", "gy", None),
        P("sec", "gx", "gy", None),
        P("sec", "gx", "gy", None),
        P("sec", "gx", "gy", None),
        P("sec", "gx", "gy"),
    )
    return jax.shard_map(
        local,
        mesh=mesh,
        in_specs=placed,
        out_specs=P("sec", None, "gx", "gy", None),
        check_vma=False,
    )
```

```python
import jax
import jax.numpy as jnp
from jax import lax
from jax.experimental import pallas as pl
from jax.experimental.pallas import tpu as pltpu
from jax.sharding import PartitionSpec as P

GAMMA_MINUS = 0.4
GAMMA_RATIO = 1.4
STEP_SIZE = 0.4
FAR = 3
NZ_DEV = 8
NY_DEV = 4
NX_DEV = 4
PLANE = NY_DEV * NX_DEV
STEPS = sorted(
    ((i, j) for i in range(NY_DEV) for j in range(NX_DEV) if i or j),
    key=lambda s: -min(s[0], NY_DEV - s[0]) - min(s[1], NX_DEV - s[1]),
)
SLOTS = 20
VMEM_BYTES = 40 * 1024 * 1024
F32 = jnp.float32
BF16 = jnp.bfloat16


def iota(shape, dim):
    return lax.broadcasted_iota(jnp.int32, shape, dim)


def two_parts(x):
    high = x.astype(BF16).astype(F32)
    return high, (x - high).astype(BF16).astype(F32)


def onehot(condition):
    return jnp.where(condition, 1.0, 0.0).astype(BF16)


def word_row(word, slot):
    base = 40 * (word // 2)
    return base + slot if word % 2 == 0 else base + 20 + (slot + 4) % 20


def pack(adjoint, cell, dest, target, weight, count):
    points = cell.shape[1]
    live = iota((1, points), 1) < count
    row, lane = cell >> 7, cell & 127
    lanes = onehot(iota((128, points), 0) == lane)
    high, low = two_parts(adjoint)
    parts = jnp.concatenate([high.astype(BF16), low.astype(BF16)], axis=1)
    picked = jnp.dot(
        parts, jnp.concatenate([lanes, lanes], axis=0), preferred_element_type=F32
    )
    row_mask = iota((64, points), 0) == row
    scale = jnp.where(live, weight, 0.0)
    words = [
        jnp.sum(
            jnp.where(row_mask, picked[64 * f : 64 * f + 64], 0.0),
            axis=0,
            keepdims=True,
        )
        * scale
        for f in range(5)
    ]
    words.append(target.astype(F32))
    place = (dest & 96) | ((dest & 3) << 3) | ((dest >> 2) & 7)
    place = jnp.where(live, place, -1)
    tiles = jnp.where(iota((128, points), 0) == place, 1.0, 0.0)
    tiles16 = tiles.astype(BF16)
    before = onehot(iota((256, 256), 0) < iota((256, 256), 1))
    ranks = []
    earlier = jnp.zeros((128, 1), F32)
    for b in range(points // 256):
        block = tiles[:, 256 * b : 256 * b + 256]
        counts = jnp.dot(
            tiles16[:, 256 * b : 256 * b + 256], before, preferred_element_type=F32
        )
        ranks.append(jnp.sum(block * (counts + earlier), axis=0, keepdims=True))
        earlier = earlier + jnp.sum(block, axis=1, keepdims=True)
    rank = jnp.concatenate(ranks, axis=1).astype(jnp.int32)
    eight = iota((8, points), 0)
    first, second, third = eight == rank, eight + 8 == rank, (eight & 3) + 16 == rank
    halves = [two_parts(w) for w in words]
    sides = []
    for side in (0, 1):
        groups = []
        for a, b in ((0, 1), (2, 3), (4, 5)):
            one, two = halves[a][side], halves[b][side]
            groups += [
                jnp.where(first, one, 0.0),
                jnp.where(second, one, 0.0),
                jnp.where(third, jnp.where(eight < 4, one, two), 0.0),
                jnp.where(first, two, 0.0),
                jnp.where(second, two, 0.0),
            ]
        groups.append(jnp.zeros((8, points), F32))
        sides.append(jnp.concatenate(groups, axis=0).astype(BF16))
    packed = lax.dot_general(
        tiles16,
        jnp.concatenate(sides, axis=0),
        (((1,), (1,)), ((), ())),
        preferred_element_type=F32,
    )
    return packed[:, :128] + packed[:, 128:]


def spread(rows, block_ref, lhs_ref, rhs_ref):
    row_iota, lane_iota = iota((32, 128), 0), iota((128, 256), 1)
    for slot in range(SLOTS):
        where = word_row(5, slot)
        target = block_ref[where : where + 1, :].astype(jnp.int32)
        row_mask = row_iota == ((target >> 7) & 31)
        target = rows[:, where : where + 1].astype(jnp.int32)
        lane = (target & 127) | ((target >> 12) << 7)
        columns = slice(128 * slot, 128 * slot + 128)
        rhs_ref[columns, :] = onehot(lane_iota == lane)
        for f in range(5):
            at = word_row(f, slot)
            high, low = two_parts(block_ref[at : at + 1, :])
            lhs_ref[32 * f : 32 * f + 32, columns] = jnp.where(
                row_mask, high, 0.0
            ).astype(BF16)
            lhs_ref[160 + 32 * f : 192 + 32 * f, columns] = jnp.where(
                row_mask, low, 0.0
            ).astype(BF16)


def differences(at):
    return (
        45.0 * (at(1) - at(-1)) - 9.0 * (at(2) - at(-2)) + (at(3) - at(-3))
    ) * (1.0 / 60.0)


def kernel(
    adjoint_hbm,
    flow_hbm,
    cell_hbm,
    dest_hbm,
    target_hbm,
    weight_hbm,
    count_hbm,
    out_ref,
    adjoint_ref,
    flow_ref,
    cell_ref,
    dest_ref,
    target_ref,
    weight_ref,
    count_ref,
    packed_ref,
    plane_ref,
    column_ref,
    near_ref,
    turned_ref,
    lhs_ref,
    rhs_ref,
    x_ref,
    y_ref,
    swap_ref,
    in_sem,
    turn_sem,
    close_sem,
    lower_sem,
    upper_sem,
    plane_send,
    plane_recv,
    near_send,
    near_recv,
    halo_send,
    halo_recv,
):
    loads = [
        pltpu.make_async_copy(src, dst, in_sem.at[i])
        for i, (src, dst) in enumerate(
            (
                (adjoint_hbm, adjoint_ref),
                (flow_hbm, flow_ref),
                (cell_hbm, cell_ref),
                (dest_hbm, dest_ref),
                (target_hbm, target_ref),
                (weight_hbm, weight_ref),
                (count_hbm, count_ref),
            )
        )
    ]
    for load in loads:
        load.start()

    sec, gx, gy = lax.axis_index("sec"), lax.axis_index("gx"), lax.axis_index("gy")
    n_gx, n_gy = lax.axis_size("gx"), lax.axis_size("gy")
    y, z = gx // NZ_DEV, gx % NZ_DEV
    is_far = sec < FAR
    is_near = sec == FAR
    core = sec % 2
    first_core = sec - core
    low_half = sec < 2
    high_half = sec >= 2
    me = y * NX_DEV + gy
    last_z = z == NZ_DEV - 1
    high_turn, low_turn = (gx < n_gx - 1) & last_z, (gx > 0) & (z == 0)

    barrier = pltpu.get_barrier_semaphore()

    def tell(condition, device):
        @pl.when(condition)
        def _():
            pl.semaphore_signal(barrier, inc=1, device_id=device)

    one, zero = jnp.int32(1), jnp.int32(0)

    def number(condition):
        return jnp.where(condition, one, zero)

    has_low, has_high = gx > 0, gx < n_gx - 1
    neighbours = (
        (has_low, {"gx": gx - 1}),
        (has_high, {"gx": gx + 1}),
        (gy > 0, {"gy": gy - 1}),
        (gy < n_gy - 1, {"gy": gy + 1}),
    )
    def plane_peer(step):
        to_y, to_x = (y + step[0]) % NY_DEV, (gy + step[1]) % NX_DEV
        return to_y * NX_DEV + to_x, {"gx": to_y * NZ_DEV + z, "gy": to_x}

    tell(low_turn, {"sec": first_core + 1, "gx": gx - 1})
    tell(high_turn, {"sec": first_core + 1, "gx": gx + jnp.where(low_half, 5, 1)})
    below = z < 4
    row = y * NZ_DEV

    @pl.when(is_near & jnp.logical_not(below))
    def _():
        for i in range(4):
            to = {"sec": 1, "gx": row + (z + i) % 4}
            pl.semaphore_signal(barrier, inc=1, device_id=to)

    @pl.when(is_near & below)
    def _():
        for i in range(3):
            to = {"sec": 1, "gx": row + 4 + i}
            pl.semaphore_signal(barrier, inc=1, device_id=to)

    @pl.when(is_near)
    def _():
        @pl.loop(0, NZ_DEV - 1)
        def _(i):
            @pl.when(i != z)
            def _():
                to = {"gx": row + i}
                pl.semaphore_signal(barrier, inc=1, device_id=to)

    @pl.when(is_far)
    def _():
        for step in STEPS:
            to = {"sec": first_core, **plane_peer(step)[1]}
            pl.semaphore_signal(barrier, inc=1, device_id=to)

    tell(has_low & (z > 0), {"sec": first_core, "gx": gx - 1})
    tell(has_high & jnp.logical_not(last_z), {"sec": first_core, "gx": gx + 1})
    tell(low_half & (z < 3), {"sec": first_core + 1, "gx": gx + 4})
    tell(low_half & (z == 3), {"sec": first_core + 1, "gx": gx + 3})
    tell(low_half & (z >= 4), {"sec": first_core + 1, "gx": gx - 4})
    tell(gy > 0, {"sec": first_core, "gy": gy - 1})
    tell(gy < n_gy - 1, {"sec": first_core, "gy": gy + 1})
    tell(core == 1, {"sec": first_core})
    tell(core == 0, {"sec": first_core + 1})
    tell(last_z, {"sec": first_core + 1, "gx": gx - 1})

    close_count = (
        2
        * (
            number(has_low & (z > 0))
            + number(has_high & jnp.logical_not(last_z))
            + number(gy > 0)
            + number(gy < n_gy - 1)
        )
        + (PLANE - 1) * jnp.where(low_half, 2, 1)
        + 1
    )
    wide_count = jnp.where(
        low_half,
        7 + 2 * number((z == 4) & (y > 0)) + 4 * number(z == NZ_DEV - 2),
        NZ_DEV + 2 * number(low_turn) + 2 * number(z == NZ_DEV - 2),
    )
    turn_count = 2 * number(high_turn) + 1

    loads[0].wait()
    loads[1].wait()

    a = [adjoint_ref[64 * f : 64 * f + 64, :] for f in range(5)]
    density, m1, m2, m3, energy, sponge = (
        flow_ref[64 * f : 64 * f + 64, :] for f in range(6)
    )
    inverse = 1.0 / density
    velocity = [m * inverse for m in (m1, m2, m3)]
    kinetic = 0.5 * (m1 * m1 + m2 * m2 + m3 * m3) * inverse
    stiffness = GAMMA_RATIO * (GAMMA_MINUS * (energy - kinetic))
    pressure_like = density * a[0] + stiffness * a[4]

    def flux(direction):
        f = [velocity[direction] * a[i] for i in range(5)]
        f[1 + direction] = f[1 + direction] + pressure_like
        f[4] = f[4] + a[1 + direction] * inverse
        return f

    for f, value in enumerate(flux(0)):
        x_ref[f, 3:11] = value.reshape(8, 8, 128)
    halos = []
    for ref, low, high in ((x_ref, 0, 1), (y_ref, 2, 3)):
        halos.append((ref, low, 3, 11, high))
        halos.append((ref, high, 8, 0, low))

    def halo_copy(i):
        ref, side, first, there, _ = halos[i]
        return pltpu.make_async_remote_copy(
            src_ref=ref.at[:, pl.ds(first, 3)],
            dst_ref=ref.at[:, pl.ds(there, 3)],
            send_sem=halo_send.at[i],
            recv_sem=halo_recv.at[i],
            device_id=neighbours[side][1],
        )

    def turn(half):
        @pl.when(half & last_z & (core == 1))
        def _():
            pl.semaphore_wait(barrier, turn_count)
            pl.semaphore_signal(turn_sem, inc=1, device_id={"sec": first_core})

        @pl.when(half & last_z & (core == 0))
        def _():
            pl.semaphore_wait(turn_sem, 1)

        @pl.when(half & high_turn)
        def _():
            halo_copy(1).start()

    turn(low_half)

    for load in loads[2:]:
        load.wait()

    @pl.when(is_far)
    def _():
        packed_ref[...] = pack(
            adjoint_ref[...],
            cell_ref[...],
            dest_ref[...],
            target_ref[...],
            weight_ref[...],
            count_ref[0, 0, 0],
        )

    for f, value in enumerate(flux(1)):
        swap_ref[64 * f : 64 * f + 64, :] = value
    for f in range(5):
        for j in range(8):
            y_ref[f, 3 + j] = swap_ref[pl.ds(64 * f + j, 8, stride=8), :]

    @pl.when(core == 0)
    def _():
        pl.semaphore_wait(barrier, close_count)
        pl.semaphore_signal(close_sem, inc=1, device_id={"sec": first_core + 1})

    @pl.when(core == 1)
    def _():
        pl.semaphore_wait(close_sem, 1)

    def own_copy():
        return pltpu.make_async_copy(
            packed_ref.at[pl.ds(pl.multiple_of(me * 8, 8), 8)],
            plane_ref.at[me],
            plane_recv,
        )

    def plane_copy(step):
        q, device = plane_peer(step)
        return pltpu.make_async_remote_copy(
            src_ref=packed_ref.at[pl.ds(pl.multiple_of(q * 8, 8), 8)],
            dst_ref=plane_ref.at[me],
            send_sem=plane_send,
            recv_sem=plane_recv,
            device_id=device,
        )

    chunk = jnp.where(low_half, 1 + z // 4, 0)
    place = jnp.where(low_half, 4 * core + z % 4, z)

    def near_copy(z_to):
        return pltpu.make_async_remote_copy(
            src_ref=column_ref.at[z_to],
            dst_ref=near_ref.at[chunk, place],
            send_sem=near_send,
            recv_sem=near_recv.at[chunk],
            device_id={"sec": FAR, "gx": y * NZ_DEV + z_to},
        )

    @pl.when(is_far)
    def _():
        own_copy().start()
        for step in STEPS:
            plane_copy(step).start()

    def start_halo(i, condition):
        @pl.when(neighbours[halos[i][1]][0] & condition)
        def _():
            halo_copy(i).start()

    start_halo(1, jnp.logical_not(last_z))
    start_halo(0, z > 0)
    for ref, _, _, there, other in halos:

        @pl.when(jnp.logical_not(neighbours[other][0]))
        def _(ref=ref, there=there):
            ref[:, there : there + 3] = jnp.zeros((5, 3, 8, 128), F32)

    flux_z = flux(2)
    for f in range(5):
        value = flux_z[f]
        along_z = differences(lambda o: pltpu.roll(value, (-o) % 128, 1))
        out_ref[64 * f : 64 * f + 64, :] = a[f] + STEP_SIZE * (along_z - sponge * a[f])

    def add_x(first, last):
        rows = 8 * (last - first)
        for f in range(5):
            along_x = differences(lambda o: x_ref[f, 3 + first + o : 3 + last + o])
            at = 64 * f + 8 * first
            out_ref[at : at + rows, :] += STEP_SIZE * along_x.reshape(rows, 128)

    add_x(3, 5)

    @pl.when((core == 1) & jnp.logical_not(last_z))
    def _():
        pl.semaphore_wait(barrier, wide_count)

        def pass_on(sem, shift):
            for to in (0, 1):
                device = {"sec": first_core + to, "gx": gx + shift}
                pl.semaphore_signal(sem, inc=1, device_id=device)

        @pl.when(low_half & below)
        def _():
            pl.semaphore_signal(upper_sem, inc=1, device_id={"sec": first_core})
            pass_on(upper_sem, 4)

        @pl.when(low_half & jnp.logical_not(below))
        def _():
            pl.semaphore_signal(lower_sem, inc=1, device_id={"sec": first_core})
            pass_on(lower_sem, -4)

        @pl.when(high_half)
        def _():
            pl.semaphore_signal(lower_sem, inc=1, device_id={"sec": first_core})

        @pl.when(z == NZ_DEV - 2)
        def _():
            pass_on(lower_sem, 1)

        @pl.when(low_half & (z == NZ_DEV - 2))
        def _():
            pass_on(lower_sem, -3)

    turn(high_half)

    @pl.when(high_half & ((core == 0) | last_z))
    def _():
        pl.semaphore_wait(lower_sem, 1)

    @pl.when(low_turn & jnp.logical_not(low_half))
    def _():
        halo_copy(0).start()

    @pl.when(is_far)
    def _():
        pltpu.make_async_copy(plane_ref, plane_ref, plane_recv).wait()
        for to in range(NZ_DEV):
            column_ref[to] = plane_ref[:, to, :]

    start_halo(2, gy >= 0)
    start_halo(3, gy >= 0)

    @pl.when(sec == 2)
    def _():
        @pl.loop(0, NZ_DEV)
        def _(j):
            near_copy(jnp.where(below, NZ_DEV - 1 - j, j)).start()

    def send_four(base, falling):
        @pl.loop(0, 4)
        def _(j):
            near_copy(base + (3 - j if falling else j)).start()

    own = (core == 1) & jnp.logical_not(last_z)

    @pl.when(low_half & below)
    def _():
        @pl.when(core == 0)
        def _():
            pl.semaphore_wait(upper_sem, 1)

        send_four(4, False)
        pl.semaphore_wait(lower_sem, 1)

        @pl.when(low_turn)
        def _():
            halo_copy(0).start()

        send_four(0, False)

    @pl.when(low_half & jnp.logical_not(below))
    def _():
        @pl.when(jnp.logical_not(own))
        def _():
            pl.semaphore_wait(lower_sem, 1)

        send_four(0, True)
        pl.semaphore_wait(upper_sem, 1)
        send_four(4, True)

    def receive(i):
        @pl.when(neighbours[halos[i][4]][0])
        def _():
            halo_copy(i).wait_recv()

    receive(2)
    receive(3)
    for f in range(5):
        along_y = differences(lambda o: y_ref[f, 3 + o : 11 + o])
        swap_ref[64 * f : 64 * f + 64, :] = along_y.reshape(64, 128)
    for f in range(5):
        for j in range(8):
            at = 64 * f + 8 * j
            out_ref[at : at + 8, :] += (
                STEP_SIZE * swap_ref[pl.ds(64 * f + j, 8, stride=8), :]
            )
    def finish_low():
        receive(1)
        add_x(0, 3)

    def finish_high():
        receive(0)
        add_x(5, 8)

    pl.when(z > 0)(finish_low)
    pl.when(jnp.logical_not(last_z))(finish_high)

    def add_points(block):
        rows = block.reshape(128, 128)
        turned_ref[...] = rows.T
        spread(rows, turned_ref, lhs_ref, rhs_ref)
        total = jnp.dot(lhs_ref[...], rhs_ref[...], preferred_element_type=F32)
        total = STEP_SIZE * (total[:160] + total[160:])
        for f in range(5):
            part = total[32 * f : 32 * f + 32]
            out_ref[64 * f : 64 * f + 32, :] += part[:, :128]
            out_ref[64 * f + 32 : 64 * f + 64, :] += part[:, 128:]

    @pl.when(is_near)
    def _():
        @pl.loop(0, FAR)
        def _(i):
            late = jnp.where(below, 0, 2)
            k = jnp.where(i == 0, 1, jnp.where(i == 1, 2 - late, late))
            pltpu.make_async_copy(
                near_ref.at[k], near_ref.at[k], near_recv.at[k]
            ).wait()
            add_points(near_ref[k])

    pl.when(z == 0)(finish_low)
    pl.when(last_z)(finish_high)

    for i in range(4):

        @pl.when(neighbours[halos[i][1]][0])
        def _(i=i):
            halo_copy(i).wait_send()

    @pl.when(is_far)
    def _():
        others = packed_ref.at[pl.ds(0, 8 * (PLANE - 1))]
        pltpu.make_async_copy(others, others, plane_send).wait()

    @pl.when(is_far)
    def _():
        pltpu.make_async_copy(column_ref, column_ref, near_send).wait()


def local(adjoint, flow, point_cell, point_dest, point_target, point_weight, point_count):
    points = point_cell.shape[-1]
    hbm = pl.BlockSpec(memory_space=pl.ANY)
    out = pl.pallas_call(
        kernel,
        out_shape=jax.ShapeDtypeStruct((320, 128), F32),
        in_specs=[hbm] * 7,
        out_specs=pl.BlockSpec(memory_space=pltpu.VMEM),
        scratch_shapes=[
            pltpu.VMEM((320, 128), F32),
            pltpu.VMEM((384, 128), F32),
            pltpu.VMEM((1, points), jnp.int32),
            pltpu.VMEM((1, points), jnp.int32),
            pltpu.VMEM((1, points), jnp.int32),
            pltpu.VMEM((1, points), F32),
            pltpu.SMEM((1, 1, 1), jnp.int32),
            pltpu.VMEM((128, 128), F32),
            pltpu.VMEM((PLANE, NZ_DEV, 128), F32),
            pltpu.VMEM((NZ_DEV, PLANE, 128), F32),
            pltpu.VMEM((FAR, NZ_DEV, PLANE, 128), F32),
            pltpu.VMEM((128, 128), F32),
            pltpu.VMEM((320, SLOTS * 128), BF16),
            pltpu.VMEM((SLOTS * 128, 256), BF16),
            pltpu.VMEM((5, 14, 8, 128), F32),
            pltpu.VMEM((5, 14, 8, 128), F32),
            pltpu.VMEM((320, 128), F32),
            pltpu.SemaphoreType.DMA((7,)),
            pltpu.SemaphoreType.REGULAR,
            pltpu.SemaphoreType.REGULAR,
            pltpu.SemaphoreType.REGULAR,
            pltpu.SemaphoreType.REGULAR,
            pltpu.SemaphoreType.DMA,
            pltpu.SemaphoreType.DMA,
            pltpu.SemaphoreType.DMA,
            pltpu.SemaphoreType.DMA((FAR,)),
            pltpu.SemaphoreType.DMA((4,)),
            pltpu.SemaphoreType.DMA((4,)),
        ],
        cost_estimate=pl.CostEstimate(
            flops=2 * 10**9, bytes_accessed=10**6, transcendentals=0
        ),
        compiler_params=pltpu.CompilerParams(
            collective_id=0, has_side_effects=True, vmem_limit_bytes=VMEM_BYTES
        ),
    )(
        *(
            pltpu.with_memory_space_constraint(v, pltpu.HBM)
            for v in (
                adjoint.reshape(320, 128),
                flow.reshape(384, 128),
                point_cell.reshape(1, points),
                point_dest.reshape(1, points),
                point_target.reshape(1, points),
                point_weight.reshape(1, points),
            )
        ),
        point_count,
    )
    return out.reshape(1, 5, 8, 8, 128)


def solution(mesh):
    placed = (
        P("sec", None, "gx", "gy", None),
        P("sec", None, "gx", "gy", None),
        P("sec", "gx", "gy", None),
        P("sec", "gx", "gy", None),
        P("sec", "gx", "gy", None),
        P("sec", "gx", "gy", None),
        P("sec", "gx", "gy"),
    )
    return jax.shard_map(
        local,
        mesh=mesh,
        in_specs=placed,
        out_specs=P("sec", None, "gx", "gy", None),
        check_vma=False,
    )
```

```python
import jax
import jax.numpy as jnp
from jax import lax
from jax.experimental import pallas as pl
from jax.experimental.pallas import tpu as pltpu
from jax.sharding import PartitionSpec as P

GAMMA_MINUS = 0.4
GAMMA_RATIO = 1.4
STEP_SIZE = 0.4
FAR = 3
NZ_DEV = 8
NY_DEV = 4
NX_DEV = 4
PLANE = NY_DEV * NX_DEV
STEPS = sorted(
    ((i, j) for i in range(NY_DEV) for j in range(NX_DEV) if i or j),
    key=lambda s: -min(s[0], NY_DEV - s[0]) - min(s[1], NX_DEV - s[1]),
)
SLOTS = 20
VMEM_BYTES = 40 * 1024 * 1024
F32 = jnp.float32
BF16 = jnp.bfloat16


def iota(shape, dim):
    return lax.broadcasted_iota(jnp.int32, shape, dim)


def two_parts(x):
    high = x.astype(BF16).astype(F32)
    return high, (x - high).astype(BF16).astype(F32)


def onehot(condition):
    return jnp.where(condition, 1.0, 0.0).astype(BF16)


def word_row(word, slot):
    base = 40 * (word // 2)
    return base + slot if word % 2 == 0 else base + 20 + (slot + 4) % 20


def pack(adjoint, cell, dest, target, weight, count):
    points = cell.shape[1]
    live = iota((1, points), 1) < count
    row, lane = cell >> 7, cell & 127
    lanes = onehot(iota((128, points), 0) == lane)
    high, low = two_parts(adjoint)
    parts = jnp.concatenate([high.astype(BF16), low.astype(BF16)], axis=1)
    picked = jnp.dot(
        parts, jnp.concatenate([lanes, lanes], axis=0), preferred_element_type=F32
    )
    row_mask = iota((64, points), 0) == row
    scale = jnp.where(live, weight, 0.0)
    words = [
        jnp.sum(
            jnp.where(row_mask, picked[64 * f : 64 * f + 64], 0.0),
            axis=0,
            keepdims=True,
        )
        * scale
        for f in range(5)
    ]
    words.append(target.astype(F32))
    place = (dest & 96) | ((dest & 3) << 3) | ((dest >> 2) & 7)
    place = jnp.where(live, place, -1)
    tiles = jnp.where(iota((128, points), 0) == place, 1.0, 0.0)
    tiles16 = tiles.astype(BF16)
    before = onehot(iota((256, 256), 0) < iota((256, 256), 1))
    ranks = []
    earlier = jnp.zeros((128, 1), F32)
    for b in range(points // 256):
        block = tiles[:, 256 * b : 256 * b + 256]
        counts = jnp.dot(
            tiles16[:, 256 * b : 256 * b + 256], before, preferred_element_type=F32
        )
        ranks.append(jnp.sum(block * (counts + earlier), axis=0, keepdims=True))
        earlier = earlier + jnp.sum(block, axis=1, keepdims=True)
    rank = jnp.concatenate(ranks, axis=1).astype(jnp.int32)
    eight = iota((8, points), 0)
    first, second, third = eight == rank, eight + 8 == rank, (eight & 3) + 16 == rank
    halves = [two_parts(w) for w in words]
    sides = []
    for side in (0, 1):
        groups = []
        for a, b in ((0, 1), (2, 3), (4, 5)):
            one, two = halves[a][side], halves[b][side]
            groups += [
                jnp.where(first, one, 0.0),
                jnp.where(second, one, 0.0),
                jnp.where(third, jnp.where(eight < 4, one, two), 0.0),
                jnp.where(first, two, 0.0),
                jnp.where(second, two, 0.0),
            ]
        groups.append(jnp.zeros((8, points), F32))
        sides.append(jnp.concatenate(groups, axis=0).astype(BF16))
    packed = lax.dot_general(
        tiles16,
        jnp.concatenate(sides, axis=0),
        (((1,), (1,)), ((), ())),
        preferred_element_type=F32,
    )
    return packed[:, :128] + packed[:, 128:]


def spread(rows, block_ref, lhs_ref, rhs_ref):
    row_iota, lane_iota = iota((32, 128), 0), iota((128, 256), 1)
    for slot in range(SLOTS):
        where = word_row(5, slot)
        target = block_ref[where : where + 1, :].astype(jnp.int32)
        row_mask = row_iota == ((target >> 7) & 31)
        target = rows[:, where : where + 1].astype(jnp.int32)
        lane = (target & 127) | ((target >> 12) << 7)
        columns = slice(128 * slot, 128 * slot + 128)
        rhs_ref[columns, :] = onehot(lane_iota == lane)
        for f in range(5):
            at = word_row(f, slot)
            high, low = two_parts(block_ref[at : at + 1, :])
            lhs_ref[32 * f : 32 * f + 32, columns] = jnp.where(
                row_mask, high, 0.0
            ).astype(BF16)
            lhs_ref[160 + 32 * f : 192 + 32 * f, columns] = jnp.where(
                row_mask, low, 0.0
            ).astype(BF16)


def differences(at):
    return (
        45.0 * (at(1) - at(-1)) - 9.0 * (at(2) - at(-2)) + (at(3) - at(-3))
    ) * (1.0 / 60.0)


def kernel(
    adjoint_hbm,
    flow_hbm,
    cell_hbm,
    dest_hbm,
    target_hbm,
    weight_hbm,
    count_hbm,
    out_ref,
    adjoint_ref,
    flow_ref,
    cell_ref,
    dest_ref,
    target_ref,
    weight_ref,
    count_ref,
    packed_ref,
    plane_ref,
    column_ref,
    near_ref,
    turned_ref,
    lhs_ref,
    rhs_ref,
    x_ref,
    y_ref,
    swap_ref,
    in_sem,
    turn_sem,
    close_sem,
    lower_sem,
    upper_sem,
    plane_send,
    plane_recv,
    near_send,
    near_recv,
    halo_send,
    halo_recv,
):
    loads = [
        pltpu.make_async_copy(src, dst, in_sem.at[i])
        for i, (src, dst) in enumerate(
            (
                (adjoint_hbm, adjoint_ref),
                (flow_hbm, flow_ref),
                (cell_hbm, cell_ref),
                (dest_hbm, dest_ref),
                (target_hbm, target_ref),
                (weight_hbm, weight_ref),
                (count_hbm, count_ref),
            )
        )
    ]
    for load in loads:
        load.start()

    sec, gx, gy = lax.axis_index("sec"), lax.axis_index("gx"), lax.axis_index("gy")
    n_gx, n_gy = lax.axis_size("gx"), lax.axis_size("gy")
    y, z = gx // NZ_DEV, gx % NZ_DEV
    is_far = sec < FAR
    is_near = sec == FAR
    core = sec % 2
    first_core = sec - core
    low_half = sec < 2
    high_half = sec >= 2
    me = y * NX_DEV + gy
    last_z = z == NZ_DEV - 1
    high_turn, low_turn = (gx < n_gx - 1) & last_z, (gx > 0) & (z == 0)

    barrier = pltpu.get_barrier_semaphore()

    def tell(condition, device):
        @pl.when(condition)
        def _():
            pl.semaphore_signal(barrier, inc=1, device_id=device)

    one, zero = jnp.int32(1), jnp.int32(0)

    def number(condition):
        return jnp.where(condition, one, zero)

    has_low, has_high = gx > 0, gx < n_gx - 1
    neighbours = (
        (has_low, {"gx": gx - 1}),
        (has_high, {"gx": gx + 1}),
        (gy > 0, {"gy": gy - 1}),
        (gy < n_gy - 1, {"gy": gy + 1}),
    )
    def plane_peer(step):
        to_y, to_x = (y + step[0]) % NY_DEV, (gy + step[1]) % NX_DEV
        return to_y * NX_DEV + to_x, {"gx": to_y * NZ_DEV + z, "gy": to_x}

    tell(low_turn, {"sec": first_core + 1, "gx": gx - 1})
    tell(high_turn, {"sec": first_core + 1, "gx": gx + jnp.where(low_half, 5, 1)})
    below = z < 4
    row = y * NZ_DEV

    @pl.when(is_near & jnp.logical_not(below))
    def _():
        for i in range(4):
            to = {"sec": 1, "gx": row + (z + i) % 4}
            pl.semaphore_signal(barrier, inc=1, device_id=to)

    @pl.when(is_near & below)
    def _():
        for i in range(3):
            to = {"sec": 1, "gx": row + 4 + i}
            pl.semaphore_signal(barrier, inc=1, device_id=to)

    @pl.when(is_near)
    def _():
        @pl.loop(0, NZ_DEV - 1)
        def _(i):
            @pl.when(i != z)
            def _():
                to = {"gx": row + i}
                pl.semaphore_signal(barrier, inc=1, device_id=to)

    @pl.when(is_far)
    def _():
        for step in STEPS:
            to = {"sec": first_core, **plane_peer(step)[1]}
            pl.semaphore_signal(barrier, inc=1, device_id=to)

    tell(has_low & (z > 0), {"sec": first_core, "gx": gx - 1})
    tell(has_high & jnp.logical_not(last_z), {"sec": first_core, "gx": gx + 1})
    tell(low_half & (z < 3), {"sec": first_core + 1, "gx": gx + 4})
    tell(low_half & (z == 3), {"sec": first_core + 1, "gx": gx + 3})
    tell(low_half & (z >= 4), {"sec": first_core + 1, "gx": gx - 4})
    tell(gy > 0, {"sec": first_core, "gy": gy - 1})
    tell(gy < n_gy - 1, {"sec": first_core, "gy": gy + 1})
    tell(core == 1, {"sec": first_core})
    tell(core == 0, {"sec": first_core + 1})
    tell(last_z, {"sec": first_core + 1, "gx": gx - 1})

    close_count = (
        2
        * (
            number(has_low & (z > 0))
            + number(has_high & jnp.logical_not(last_z))
            + number(gy > 0)
            + number(gy < n_gy - 1)
        )
        + (PLANE - 1) * jnp.where(low_half, 2, 1)
        + 1
    )
    wide_count = jnp.where(
        low_half,
        7 + 2 * number((z == 4) & (y > 0)) + 4 * number(z == NZ_DEV - 2),
        NZ_DEV + 2 * number(low_turn) + 2 * number(z == NZ_DEV - 2),
    )
    turn_count = 2 * number(high_turn) + 1

    loads[0].wait()
    loads[1].wait()

    a = [adjoint_ref[64 * f : 64 * f + 64, :] for f in range(5)]
    density, m1, m2, m3, energy, sponge = (
        flow_ref[64 * f : 64 * f + 64, :] for f in range(6)
    )
    inverse = 1.0 / density
    velocity = [m * inverse for m in (m1, m2, m3)]
    kinetic = 0.5 * (m1 * m1 + m2 * m2 + m3 * m3) * inverse
    stiffness = GAMMA_RATIO * (GAMMA_MINUS * (energy - kinetic))
    pressure_like = density * a[0] + stiffness * a[4]

    def flux(direction):
        f = [velocity[direction] * a[i] for i in range(5)]
        f[1 + direction] = f[1 + direction] + pressure_like
        f[4] = f[4] + a[1 + direction] * inverse
        return f

    for f, value in enumerate(flux(0)):
        x_ref[f, 3:11] = value.reshape(8, 8, 128)
    halos = []
    for ref, low, high in ((x_ref, 0, 1), (y_ref, 2, 3)):
        halos.append((ref, low, 3, 11, high))
        halos.append((ref, high, 8, 0, low))

    def halo_copy(i):
        ref, side, first, there, _ = halos[i]
        return pltpu.make_async_remote_copy(
            src_ref=ref.at[:, pl.ds(first, 3)],
            dst_ref=ref.at[:, pl.ds(there, 3)],
            send_sem=halo_send.at[i],
            recv_sem=halo_recv.at[i],
            device_id=neighbours[side][1],
        )

    def turn(half):
        @pl.when(half & last_z & (core == 1))
        def _():
            pl.semaphore_wait(barrier, turn_count)
            pl.semaphore_signal(turn_sem, inc=1, device_id={"sec": first_core})

        @pl.when(half & last_z & (core == 0))
        def _():
            pl.semaphore_wait(turn_sem, 1)

        @pl.when(half & high_turn)
        def _():
            halo_copy(1).start()

    turn(low_half)

    for load in loads[2:]:
        load.wait()

    @pl.when(is_far)
    def _():
        packed_ref[...] = pack(
            adjoint_ref[...],
            cell_ref[...],
            dest_ref[...],
            target_ref[...],
            weight_ref[...],
            count_ref[0, 0, 0],
        )

    for f, value in enumerate(flux(1)):
        swap_ref[64 * f : 64 * f + 64, :] = value
    for f in range(5):
        for j in range(8):
            y_ref[f, 3 + j] = swap_ref[pl.ds(64 * f + j, 8, stride=8), :]

    @pl.when(core == 0)
    def _():
        pl.semaphore_wait(barrier, close_count)
        pl.semaphore_signal(close_sem, inc=1, device_id={"sec": first_core + 1})

    @pl.when(core == 1)
    def _():
        pl.semaphore_wait(close_sem, 1)

    def own_copy():
        return pltpu.make_async_copy(
            packed_ref.at[pl.ds(pl.multiple_of(me * 8, 8), 8)],
            plane_ref.at[me],
            plane_recv,
        )

    def plane_copy(step):
        q, device = plane_peer(step)
        return pltpu.make_async_remote_copy(
            src_ref=packed_ref.at[pl.ds(pl.multiple_of(q * 8, 8), 8)],
            dst_ref=plane_ref.at[me],
            send_sem=plane_send,
            recv_sem=plane_recv,
            device_id=device,
        )

    chunk = jnp.where(low_half, 1 + z // 4, 0)
    place = jnp.where(low_half, 4 * core + z % 4, z)

    def near_copy(z_to):
        return pltpu.make_async_remote_copy(
            src_ref=column_ref.at[z_to],
            dst_ref=near_ref.at[chunk, place],
            send_sem=near_send,
            recv_sem=near_recv.at[chunk],
            device_id={"sec": FAR, "gx": y * NZ_DEV + z_to},
        )

    @pl.when(is_far)
    def _():
        own_copy().start()
        for step in STEPS:
            plane_copy(step).start()

    def start_halo(i, condition):
        @pl.when(neighbours[halos[i][1]][0] & condition)
        def _():
            halo_copy(i).start()

    start_halo(1, jnp.logical_not(last_z))
    start_halo(0, z > 0)
    for ref, _, _, there, other in halos:

        @pl.when(jnp.logical_not(neighbours[other][0]))
        def _(ref=ref, there=there):
            ref[:, there : there + 3] = jnp.zeros((5, 3, 8, 128), F32)

    flux_z = flux(2)
    for f in range(5):
        value = flux_z[f]
        along_z = differences(lambda o: pltpu.roll(value, (-o) % 128, 1))
        out_ref[64 * f : 64 * f + 64, :] = a[f] + STEP_SIZE * (along_z - sponge * a[f])

    def add_x(first, last):
        rows = 8 * (last - first)
        for f in range(5):
            along_x = differences(lambda o: x_ref[f, 3 + first + o : 3 + last + o])
            at = 64 * f + 8 * first
            out_ref[at : at + rows, :] += STEP_SIZE * along_x.reshape(rows, 128)

    add_x(3, 5)

    @pl.when((core == 1) & jnp.logical_not(last_z))
    def _():
        pl.semaphore_wait(barrier, wide_count)

        def pass_on(sem, shift):
            for to in (0, 1):
                device = {"sec": first_core + to, "gx": gx + shift}
                pl.semaphore_signal(sem, inc=1, device_id=device)

        @pl.when(low_half & below)
        def _():
            pl.semaphore_signal(upper_sem, inc=1, device_id={"sec": first_core})
            pass_on(upper_sem, 4)

        @pl.when(low_half & jnp.logical_not(below))
        def _():
            pl.semaphore_signal(lower_sem, inc=1, device_id={"sec": first_core})
            pass_on(lower_sem, -4)

        @pl.when(high_half)
        def _():
            pl.semaphore_signal(lower_sem, inc=1, device_id={"sec": first_core})

        @pl.when(z == NZ_DEV - 2)
        def _():
            pass_on(lower_sem, 1)

        @pl.when(low_half & (z == NZ_DEV - 2))
        def _():
            pass_on(lower_sem, -3)

    turn(high_half)

    @pl.when(high_half & ((core == 0) | last_z))
    def _():
        pl.semaphore_wait(lower_sem, 1)

    @pl.when(low_turn & jnp.logical_not(low_half))
    def _():
        halo_copy(0).start()

    @pl.when(is_far)
    def _():
        pltpu.make_async_copy(plane_ref, plane_ref, plane_recv).wait()
        for to in range(NZ_DEV):
            column_ref[to] = plane_ref[:, to, :]

    start_halo(2, gy >= 0)
    start_halo(3, gy >= 0)

    @pl.when(sec == 2)
    def _():
        @pl.loop(0, NZ_DEV)
        def _(j):
            near_copy(jnp.where(below, NZ_DEV - 1 - j, j)).start()

    def send_four(base, falling):
        @pl.loop(0, 4)
        def _(j):
            near_copy(base + (3 - j if falling else j)).start()

    own = (core == 1) & jnp.logical_not(last_z)

    @pl.when(low_half & below)
    def _():
        @pl.when(core == 0)
        def _():
            pl.semaphore_wait(upper_sem, 1)

        send_four(4, False)
        pl.semaphore_wait(lower_sem, 1)

        @pl.when(low_turn)
        def _():
            halo_copy(0).start()

        send_four(0, False)

    @pl.when(low_half & jnp.logical_not(below))
    def _():
        @pl.when(jnp.logical_not(own))
        def _():
            pl.semaphore_wait(lower_sem, 1)

        pl.semaphore_wait(upper_sem, 1)
        send_four(4, True)
        send_four(0, True)

    def receive(i):
        @pl.when(neighbours[halos[i][4]][0])
        def _():
            halo_copy(i).wait_recv()

    receive(2)
    receive(3)
    for f in range(5):
        along_y = differences(lambda o: y_ref[f, 3 + o : 11 + o])
        swap_ref[64 * f : 64 * f + 64, :] = along_y.reshape(64, 128)
    for f in range(5):
        for j in range(8):
            at = 64 * f + 8 * j
            out_ref[at : at + 8, :] += (
                STEP_SIZE * swap_ref[pl.ds(64 * f + j, 8, stride=8), :]
            )
    def finish_low():
        receive(1)
        add_x(0, 3)

    def finish_high():
        receive(0)
        add_x(5, 8)

    pl.when(z > 0)(finish_low)
    pl.when(jnp.logical_not(last_z))(finish_high)

    def add_points(block):
        rows = block.reshape(128, 128)
        turned_ref[...] = rows.T
        spread(rows, turned_ref, lhs_ref, rhs_ref)
        total = jnp.dot(lhs_ref[...], rhs_ref[...], preferred_element_type=F32)
        total = STEP_SIZE * (total[:160] + total[160:])
        for f in range(5):
            part = total[32 * f : 32 * f + 32]
            out_ref[64 * f : 64 * f + 32, :] += part[:, :128]
            out_ref[64 * f + 32 : 64 * f + 64, :] += part[:, 128:]

    @pl.when(is_near)
    def _():
        @pl.loop(0, FAR)
        def _(i):
            late = jnp.where(below, 0, 2)
            k = jnp.where(i == 0, 1, jnp.where(i == 1, 2 - late, late))
            pltpu.make_async_copy(
                near_ref.at[k], near_ref.at[k], near_recv.at[k]
            ).wait()
            add_points(near_ref[k])

    pl.when(z == 0)(finish_low)
    pl.when(last_z)(finish_high)

    for i in range(4):

        @pl.when(neighbours[halos[i][1]][0])
        def _(i=i):
            halo_copy(i).wait_send()

    @pl.when(is_far)
    def _():
        others = packed_ref.at[pl.ds(0, 8 * (PLANE - 1))]
        pltpu.make_async_copy(others, others, plane_send).wait()

    @pl.when(is_far)
    def _():
        pltpu.make_async_copy(column_ref, column_ref, near_send).wait()


def local(adjoint, flow, point_cell, point_dest, point_target, point_weight, point_count):
    points = point_cell.shape[-1]
    hbm = pl.BlockSpec(memory_space=pl.ANY)
    out = pl.pallas_call(
        kernel,
        out_shape=jax.ShapeDtypeStruct((320, 128), F32),
        in_specs=[hbm] * 7,
        out_specs=pl.BlockSpec(memory_space=pltpu.VMEM),
        scratch_shapes=[
            pltpu.VMEM((320, 128), F32),
            pltpu.VMEM((384, 128), F32),
            pltpu.VMEM((1, points), jnp.int32),
            pltpu.VMEM((1, points), jnp.int32),
            pltpu.VMEM((1, points), jnp.int32),
            pltpu.VMEM((1, points), F32),
            pltpu.SMEM((1, 1, 1), jnp.int32),
            pltpu.VMEM((128, 128), F32),
            pltpu.VMEM((PLANE, NZ_DEV, 128), F32),
            pltpu.VMEM((NZ_DEV, PLANE, 128), F32),
            pltpu.VMEM((FAR, NZ_DEV, PLANE, 128), F32),
            pltpu.VMEM((128, 128), F32),
            pltpu.VMEM((320, SLOTS * 128), BF16),
            pltpu.VMEM((SLOTS * 128, 256), BF16),
            pltpu.VMEM((5, 14, 8, 128), F32),
            pltpu.VMEM((5, 14, 8, 128), F32),
            pltpu.VMEM((320, 128), F32),
            pltpu.SemaphoreType.DMA((7,)),
            pltpu.SemaphoreType.REGULAR,
            pltpu.SemaphoreType.REGULAR,
            pltpu.SemaphoreType.REGULAR,
            pltpu.SemaphoreType.REGULAR,
            pltpu.SemaphoreType.DMA,
            pltpu.SemaphoreType.DMA,
            pltpu.SemaphoreType.DMA,
            pltpu.SemaphoreType.DMA((FAR,)),
            pltpu.SemaphoreType.DMA((4,)),
            pltpu.SemaphoreType.DMA((4,)),
        ],
        cost_estimate=pl.CostEstimate(
            flops=2 * 10**9, bytes_accessed=10**6, transcendentals=0
        ),
        compiler_params=pltpu.CompilerParams(
            collective_id=0, has_side_effects=True, vmem_limit_bytes=VMEM_BYTES
        ),
    )(
        *(
            pltpu.with_memory_space_constraint(v, pltpu.HBM)
            for v in (
                adjoint.reshape(320, 128),
                flow.reshape(384, 128),
                point_cell.reshape(1, points),
                point_dest.reshape(1, points),
                point_target.reshape(1, points),
                point_weight.reshape(1, points),
            )
        ),
        point_count,
    )
    return out.reshape(1, 5, 8, 8, 128)


def solution(mesh):
    placed = (
        P("sec", None, "gx", "gy", None),
        P("sec", None, "gx", "gy", None),
        P("sec", "gx", "gy", None),
        P("sec", "gx", "gy", None),
        P("sec", "gx", "gy", None),
        P("sec", "gx", "gy", None),
        P("sec", "gx", "gy"),
    )
    return jax.shard_map(
        local,
        mesh=mesh,
        in_specs=placed,
        out_specs=P("sec", None, "gx", "gy", None),
        check_vma=False,
    )
```

```python
import jax
import jax.numpy as jnp
from jax import lax
from jax.experimental import pallas as pl
from jax.experimental.pallas import tpu as pltpu
from jax.sharding import PartitionSpec as P

GAMMA_MINUS = 0.4
GAMMA_RATIO = 1.4
STEP_SIZE = 0.4
FAR = 3
NZ_DEV = 8
NY_DEV = 4
NX_DEV = 4
PLANE = NY_DEV * NX_DEV
STEPS = sorted(
    ((i, j) for i in range(NY_DEV) for j in range(NX_DEV) if i or j),
    key=lambda s: -min(s[0], NY_DEV - s[0]) - min(s[1], NX_DEV - s[1]),
)
SLOTS = 20
VMEM_BYTES = 40 * 1024 * 1024
F32 = jnp.float32
BF16 = jnp.bfloat16


def iota(shape, dim):
    return lax.broadcasted_iota(jnp.int32, shape, dim)


def two_parts(x):
    high = x.astype(BF16).astype(F32)
    return high, (x - high).astype(BF16).astype(F32)


def onehot(condition):
    return jnp.where(condition, 1.0, 0.0).astype(BF16)


def word_row(word, slot):
    base = 40 * (word // 2)
    return base + slot if word % 2 == 0 else base + 20 + (slot + 4) % 20


def pack(adjoint, cell, dest, target, weight, count):
    points = cell.shape[1]
    live = iota((1, points), 1) < count
    row, lane = cell >> 7, cell & 127
    lanes = onehot(iota((128, points), 0) == lane)
    high, low = two_parts(adjoint)
    parts = jnp.concatenate([high.astype(BF16), low.astype(BF16)], axis=1)
    picked = jnp.dot(
        parts, jnp.concatenate([lanes, lanes], axis=0), preferred_element_type=F32
    )
    row_mask = iota((64, points), 0) == row
    scale = jnp.where(live, weight, 0.0)
    words = [
        jnp.sum(
            jnp.where(row_mask, picked[64 * f : 64 * f + 64], 0.0),
            axis=0,
            keepdims=True,
        )
        * scale
        for f in range(5)
    ]
    words.append(target.astype(F32))
    place = (dest & 96) | ((dest & 3) << 3) | ((dest >> 2) & 7)
    place = jnp.where(live, place, -1)
    tiles = jnp.where(iota((128, points), 0) == place, 1.0, 0.0)
    tiles16 = tiles.astype(BF16)
    before = onehot(iota((256, 256), 0) < iota((256, 256), 1))
    ranks = []
    earlier = jnp.zeros((128, 1), F32)
    for b in range(points // 256):
        block = tiles[:, 256 * b : 256 * b + 256]
        counts = jnp.dot(
            tiles16[:, 256 * b : 256 * b + 256], before, preferred_element_type=F32
        )
        ranks.append(jnp.sum(block * (counts + earlier), axis=0, keepdims=True))
        earlier = earlier + jnp.sum(block, axis=1, keepdims=True)
    rank = jnp.concatenate(ranks, axis=1).astype(jnp.int32)
    eight = iota((8, points), 0)
    first, second, third = eight == rank, eight + 8 == rank, (eight & 3) + 16 == rank
    halves = [two_parts(w) for w in words]
    sides = []
    for side in (0, 1):
        groups = []
        for a, b in ((0, 1), (2, 3), (4, 5)):
            one, two = halves[a][side], halves[b][side]
            groups += [
                jnp.where(first, one, 0.0),
                jnp.where(second, one, 0.0),
                jnp.where(third, jnp.where(eight < 4, one, two), 0.0),
                jnp.where(first, two, 0.0),
                jnp.where(second, two, 0.0),
            ]
        groups.append(jnp.zeros((8, points), F32))
        sides.append(jnp.concatenate(groups, axis=0).astype(BF16))
    packed = lax.dot_general(
        tiles16,
        jnp.concatenate(sides, axis=0),
        (((1,), (1,)), ((), ())),
        preferred_element_type=F32,
    )
    return packed[:, :128] + packed[:, 128:]


def spread(slots, rows, block_ref, lhs_ref, rhs_ref):
    row_iota, lane_iota = iota((32, 128), 0), iota((128, 256), 1)
    for slot in slots:
        where = word_row(5, slot)
        target = block_ref[where : where + 1, :].astype(jnp.int32)
        row_mask = row_iota == ((target >> 7) & 31)
        target = rows[:, where : where + 1].astype(jnp.int32)
        lane = (target & 127) | ((target >> 12) << 7)
        columns = slice(128 * slot, 128 * slot + 128)
        rhs_ref[columns, :] = onehot(lane_iota == lane)
        for f in range(5):
            at = word_row(f, slot)
            high, low = two_parts(block_ref[at : at + 1, :])
            lhs_ref[32 * f : 32 * f + 32, columns] = jnp.where(
                row_mask, high, 0.0
            ).astype(BF16)
            lhs_ref[160 + 32 * f : 192 + 32 * f, columns] = jnp.where(
                row_mask, low, 0.0
            ).astype(BF16)


def differences(at):
    return (
        45.0 * (at(1) - at(-1)) - 9.0 * (at(2) - at(-2)) + (at(3) - at(-3))
    ) * (1.0 / 60.0)


def kernel(
    adjoint_hbm,
    flow_hbm,
    cell_hbm,
    dest_hbm,
    target_hbm,
    weight_hbm,
    count_hbm,
    out_ref,
    adjoint_ref,
    flow_ref,
    cell_ref,
    dest_ref,
    target_ref,
    weight_ref,
    count_ref,
    packed_ref,
    plane_ref,
    column_ref,
    near_ref,
    turned_ref,
    lhs_ref,
    rhs_ref,
    x_ref,
    y_ref,
    swap_ref,
    in_sem,
    turn_sem,
    close_sem,
    lower_sem,
    upper_sem,
    plane_send,
    plane_recv,
    near_send,
    near_recv,
    halo_send,
    halo_recv,
):
    loads = [
        pltpu.make_async_copy(src, dst, in_sem.at[i])
        for i, (src, dst) in enumerate(
            (
                (adjoint_hbm, adjoint_ref),
                (flow_hbm, flow_ref),
                (cell_hbm, cell_ref),
                (dest_hbm, dest_ref),
                (target_hbm, target_ref),
                (weight_hbm, weight_ref),
                (count_hbm, count_ref),
            )
        )
    ]
    for load in loads:
        load.start()

    sec, gx, gy = lax.axis_index("sec"), lax.axis_index("gx"), lax.axis_index("gy")
    n_gx, n_gy = lax.axis_size("gx"), lax.axis_size("gy")
    y, z = gx // NZ_DEV, gx % NZ_DEV
    is_far = sec < FAR
    is_near = sec == FAR
    core = sec % 2
    first_core = sec - core
    low_half = sec < 2
    high_half = sec >= 2
    me = y * NX_DEV + gy
    last_z = z == NZ_DEV - 1
    high_turn, low_turn = (gx < n_gx - 1) & last_z, (gx > 0) & (z == 0)

    barrier = pltpu.get_barrier_semaphore()

    def tell(condition, device):
        @pl.when(condition)
        def _():
            pl.semaphore_signal(barrier, inc=1, device_id=device)

    one, zero = jnp.int32(1), jnp.int32(0)

    def number(condition):
        return jnp.where(condition, one, zero)

    has_low, has_high = gx > 0, gx < n_gx - 1
    neighbours = (
        (has_low, {"gx": gx - 1}),
        (has_high, {"gx": gx + 1}),
        (gy > 0, {"gy": gy - 1}),
        (gy < n_gy - 1, {"gy": gy + 1}),
    )
    def plane_peer(step):
        to_y, to_x = (y + step[0]) % NY_DEV, (gy + step[1]) % NX_DEV
        return to_y * NX_DEV + to_x, {"gx": to_y * NZ_DEV + z, "gy": to_x}

    tell(low_turn, {"sec": first_core + 1, "gx": gx - 1})
    tell(high_turn, {"sec": first_core + 1, "gx": gx + jnp.where(low_half, 5, 1)})
    below = z < 4
    row = y * NZ_DEV

    @pl.when(is_near & jnp.logical_not(below))
    def _():
        for i in range(4):
            to = {"sec": 1, "gx": row + (z + i) % 4}
            pl.semaphore_signal(barrier, inc=1, device_id=to)

    @pl.when(is_near & below)
    def _():
        for i in range(3):
            to = {"sec": 1, "gx": row + 4 + i}
            pl.semaphore_signal(barrier, inc=1, device_id=to)

    @pl.when(is_near)
    def _():
        @pl.loop(0, NZ_DEV - 1)
        def _(i):
            @pl.when(i != z)
            def _():
                to = {"gx": row + i}
                pl.semaphore_signal(barrier, inc=1, device_id=to)

    @pl.when(is_far)
    def _():
        for step in STEPS:
            to = {"sec": first_core, **plane_peer(step)[1]}
            pl.semaphore_signal(barrier, inc=1, device_id=to)

    tell(has_low & (z > 0), {"sec": first_core, "gx": gx - 1})
    tell(has_high & jnp.logical_not(last_z), {"sec": first_core, "gx": gx + 1})
    tell(low_half & (z < 3), {"sec": first_core + 1, "gx": gx + 4})
    tell(low_half & (z == 3), {"sec": first_core + 1, "gx": gx + 3})
    tell(low_half & (z >= 4), {"sec": first_core + 1, "gx": gx - 4})
    tell(gy > 0, {"sec": first_core, "gy": gy - 1})
    tell(gy < n_gy - 1, {"sec": first_core, "gy": gy + 1})
    tell(core == 1, {"sec": first_core})
    tell(core == 0, {"sec": first_core + 1})
    tell(last_z, {"sec": first_core + 1, "gx": gx - 1})

    close_count = (
        2
        * (
            number(has_low & (z > 0))
            + number(has_high & jnp.logical_not(last_z))
            + number(gy > 0)
            + number(gy < n_gy - 1)
        )
        + (PLANE - 1) * jnp.where(low_half, 2, 1)
        + 1
    )
    wide_count = jnp.where(
        low_half,
        7 + 2 * number((z == 4) & (y > 0)) + 4 * number(z == NZ_DEV - 2),
        NZ_DEV + 2 * number(low_turn) + 2 * number(z == NZ_DEV - 2),
    )
    turn_count = 2 * number(high_turn) + 1

    loads[0].wait()
    loads[1].wait()

    a = [adjoint_ref[64 * f : 64 * f + 64, :] for f in range(5)]
    density, m1, m2, m3, energy, sponge = (
        flow_ref[64 * f : 64 * f + 64, :] for f in range(6)
    )
    inverse = 1.0 / density
    velocity = [m * inverse for m in (m1, m2, m3)]
    kinetic = 0.5 * (m1 * m1 + m2 * m2 + m3 * m3) * inverse
    stiffness = GAMMA_RATIO * (GAMMA_MINUS * (energy - kinetic))
    pressure_like = density * a[0] + stiffness * a[4]

    def flux(direction):
        f = [velocity[direction] * a[i] for i in range(5)]
        f[1 + direction] = f[1 + direction] + pressure_like
        f[4] = f[4] + a[1 + direction] * inverse
        return f

    for f, value in enumerate(flux(0)):
        x_ref[f, 3:11] = value.reshape(8, 8, 128)
    halos = []
    for ref, low, high in ((x_ref, 0, 1), (y_ref, 2, 3)):
        halos.append((ref, low, 3, 11, high))
        halos.append((ref, high, 8, 0, low))

    def halo_copy(i):
        ref, side, first, there, _ = halos[i]
        return pltpu.make_async_remote_copy(
            src_ref=ref.at[:, pl.ds(first, 3)],
            dst_ref=ref.at[:, pl.ds(there, 3)],
            send_sem=halo_send.at[i],
            recv_sem=halo_recv.at[i],
            device_id=neighbours[side][1],
        )

    def turn(half):
        @pl.when(half & last_z & (core == 1))
        def _():
            pl.semaphore_wait(barrier, turn_count)
            pl.semaphore_signal(turn_sem, inc=1, device_id={"sec": first_core})

        @pl.when(half & last_z & (core == 0))
        def _():
            pl.semaphore_wait(turn_sem, 1)

        @pl.when(half & high_turn)
        def _():
            halo_copy(1).start()

    turn(low_half)

    for load in loads[2:]:
        load.wait()

    @pl.when(is_far)
    def _():
        packed_ref[...] = pack(
            adjoint_ref[...],
            cell_ref[...],
            dest_ref[...],
            target_ref[...],
            weight_ref[...],
            count_ref[0, 0, 0],
        )

    for f, value in enumerate(flux(1)):
        swap_ref[64 * f : 64 * f + 64, :] = value
    for f in range(5):
        for j in range(8):
            y_ref[f, 3 + j] = swap_ref[pl.ds(64 * f + j, 8, stride=8), :]

    @pl.when(core == 0)
    def _():
        pl.semaphore_wait(barrier, close_count)
        pl.semaphore_signal(close_sem, inc=1, device_id={"sec": first_core + 1})

    @pl.when(core == 1)
    def _():
        pl.semaphore_wait(close_sem, 1)

    def own_copy():
        return pltpu.make_async_copy(
            packed_ref.at[pl.ds(pl.multiple_of(me * 8, 8), 8)],
            plane_ref.at[me],
            plane_recv,
        )

    def plane_copy(step):
        q, device = plane_peer(step)
        return pltpu.make_async_remote_copy(
            src_ref=packed_ref.at[pl.ds(pl.multiple_of(q * 8, 8), 8)],
            dst_ref=plane_ref.at[me],
            send_sem=plane_send,
            recv_sem=plane_recv,
            device_id=device,
        )

    chunk = jnp.where(low_half, 1 + z // 4, 0)
    place = jnp.where(low_half, 4 * core + z % 4, z)

    def near_copy(z_to):
        return pltpu.make_async_remote_copy(
            src_ref=column_ref.at[z_to],
            dst_ref=near_ref.at[chunk, place],
            send_sem=near_send,
            recv_sem=near_recv.at[chunk],
            device_id={"sec": FAR, "gx": y * NZ_DEV + z_to},
        )

    @pl.when(is_far)
    def _():
        own_copy().start()
        for step in STEPS:
            plane_copy(step).start()

    def start_halo(i, condition):
        @pl.when(neighbours[halos[i][1]][0] & condition)
        def _():
            halo_copy(i).start()

    start_halo(1, jnp.logical_not(last_z))
    start_halo(0, z > 0)
    for ref, _, _, there, other in halos:

        @pl.when(jnp.logical_not(neighbours[other][0]))
        def _(ref=ref, there=there):
            ref[:, there : there + 3] = jnp.zeros((5, 3, 8, 128), F32)

    flux_z = flux(2)
    for f in range(5):
        value = flux_z[f]
        along_z = differences(lambda o: pltpu.roll(value, (-o) % 128, 1))
        out_ref[64 * f : 64 * f + 64, :] = a[f] + STEP_SIZE * (along_z - sponge * a[f])

    def add_x(first, last):
        rows = 8 * (last - first)
        for f in range(5):
            along_x = differences(lambda o: x_ref[f, 3 + first + o : 3 + last + o])
            at = 64 * f + 8 * first
            out_ref[at : at + rows, :] += STEP_SIZE * along_x.reshape(rows, 128)

    add_x(3, 5)

    @pl.when((core == 1) & jnp.logical_not(last_z))
    def _():
        pl.semaphore_wait(barrier, wide_count)

        def pass_on(sem, shift):
            for to in (0, 1):
                device = {"sec": first_core + to, "gx": gx + shift}
                pl.semaphore_signal(sem, inc=1, device_id=device)

        @pl.when(low_half & below)
        def _():
            pl.semaphore_signal(upper_sem, inc=1, device_id={"sec": first_core})
            pass_on(upper_sem, 4)

        @pl.when(low_half & jnp.logical_not(below))
        def _():
            pl.semaphore_signal(lower_sem, inc=1, device_id={"sec": first_core})
            pass_on(lower_sem, -4)

        @pl.when(high_half)
        def _():
            pl.semaphore_signal(lower_sem, inc=1, device_id={"sec": first_core})

        @pl.when(z == NZ_DEV - 2)
        def _():
            pass_on(lower_sem, 1)

        @pl.when(low_half & (z == NZ_DEV - 2))
        def _():
            pass_on(lower_sem, -3)

    turn(high_half)

    @pl.when(high_half & ((core == 0) | last_z))
    def _():
        pl.semaphore_wait(lower_sem, 1)

    @pl.when(low_turn & jnp.logical_not(low_half))
    def _():
        halo_copy(0).start()

    @pl.when(is_far)
    def _():
        pltpu.make_async_copy(plane_ref, plane_ref, plane_recv).wait()
        for to in range(NZ_DEV):
            column_ref[to] = plane_ref[:, to, :]

    start_halo(2, gy >= 0)
    start_halo(3, gy >= 0)

    @pl.when(sec == 2)
    def _():
        @pl.loop(0, NZ_DEV)
        def _(j):
            near_copy(jnp.where(below, NZ_DEV - 1 - j, j)).start()

    def send_four(base, falling):
        @pl.loop(0, 4)
        def _(j):
            near_copy(base + (3 - j if falling else j)).start()

    own = (core == 1) & jnp.logical_not(last_z)

    @pl.when(low_half & below)
    def _():
        @pl.when(core == 0)
        def _():
            pl.semaphore_wait(upper_sem, 1)

        send_four(4, False)
        pl.semaphore_wait(lower_sem, 1)

        @pl.when(low_turn)
        def _():
            halo_copy(0).start()

        send_four(0, False)

    @pl.when(low_half & jnp.logical_not(below))
    def _():
        @pl.when(jnp.logical_not(own))
        def _():
            pl.semaphore_wait(lower_sem, 1)

        pl.semaphore_wait(upper_sem, 1)
        send_four(4, True)
        send_four(0, True)

    def receive(i):
        @pl.when(neighbours[halos[i][4]][0])
        def _():
            halo_copy(i).wait_recv()

    receive(2)
    receive(3)
    for f in range(5):
        along_y = differences(lambda o: y_ref[f, 3 + o : 11 + o])
        swap_ref[64 * f : 64 * f + 64, :] = along_y.reshape(64, 128)
    for f in range(5):
        for j in range(8):
            at = 64 * f + 8 * j
            out_ref[at : at + 8, :] += (
                STEP_SIZE * swap_ref[pl.ds(64 * f + j, 8, stride=8), :]
            )
    def finish_low():
        receive(1)
        add_x(0, 3)

    def finish_high():
        receive(0)
        add_x(5, 8)

    pl.when(z > 0)(finish_low)
    pl.when(jnp.logical_not(last_z))(finish_high)

    def add_points(block):
        rows = block.reshape(128, 128)
        turned_ref[...] = rows.T
        total = 0.0
        for first in (0, SLOTS // 2):
            slots = range(first, first + SLOTS // 2)
            spread(slots, rows, turned_ref, lhs_ref, rhs_ref)
            part = slice(128 * first, 128 * (first + SLOTS // 2))
            total += jnp.dot(
                lhs_ref[:, part], rhs_ref[part, :], preferred_element_type=F32
            )
        total = STEP_SIZE * (total[:160] + total[160:])
        for f in range(5):
            part = total[32 * f : 32 * f + 32]
            out_ref[64 * f : 64 * f + 32, :] += part[:, :128]
            out_ref[64 * f + 32 : 64 * f + 64, :] += part[:, 128:]

    @pl.when(is_near)
    def _():
        @pl.loop(0, FAR)
        def _(i):
            late = jnp.where(below, 0, 2)
            k = jnp.where(i == 0, 1, jnp.where(i == 1, 2 - late, late))
            pltpu.make_async_copy(
                near_ref.at[k], near_ref.at[k], near_recv.at[k]
            ).wait()
            add_points(near_ref[k])

    pl.when(z == 0)(finish_low)
    pl.when(last_z)(finish_high)

    for i in range(4):

        @pl.when(neighbours[halos[i][1]][0])
        def _(i=i):
            halo_copy(i).wait_send()

    @pl.when(is_far)
    def _():
        others = packed_ref.at[pl.ds(0, 8 * (PLANE - 1))]
        pltpu.make_async_copy(others, others, plane_send).wait()

    @pl.when(is_far)
    def _():
        pltpu.make_async_copy(column_ref, column_ref, near_send).wait()


def local(adjoint, flow, point_cell, point_dest, point_target, point_weight, point_count):
    points = point_cell.shape[-1]
    hbm = pl.BlockSpec(memory_space=pl.ANY)
    out = pl.pallas_call(
        kernel,
        out_shape=jax.ShapeDtypeStruct((320, 128), F32),
        in_specs=[hbm] * 7,
        out_specs=pl.BlockSpec(memory_space=pltpu.VMEM),
        scratch_shapes=[
            pltpu.VMEM((320, 128), F32),
            pltpu.VMEM((384, 128), F32),
            pltpu.VMEM((1, points), jnp.int32),
            pltpu.VMEM((1, points), jnp.int32),
            pltpu.VMEM((1, points), jnp.int32),
            pltpu.VMEM((1, points), F32),
            pltpu.SMEM((1, 1, 1), jnp.int32),
            pltpu.VMEM((128, 128), F32),
            pltpu.VMEM((PLANE, NZ_DEV, 128), F32),
            pltpu.VMEM((NZ_DEV, PLANE, 128), F32),
            pltpu.VMEM((FAR, NZ_DEV, PLANE, 128), F32),
            pltpu.VMEM((128, 128), F32),
            pltpu.VMEM((320, SLOTS * 128), BF16),
            pltpu.VMEM((SLOTS * 128, 256), BF16),
            pltpu.VMEM((5, 14, 8, 128), F32),
            pltpu.VMEM((5, 14, 8, 128), F32),
            pltpu.VMEM((320, 128), F32),
            pltpu.SemaphoreType.DMA((7,)),
            pltpu.SemaphoreType.REGULAR,
            pltpu.SemaphoreType.REGULAR,
            pltpu.SemaphoreType.REGULAR,
            pltpu.SemaphoreType.REGULAR,
            pltpu.SemaphoreType.DMA,
            pltpu.SemaphoreType.DMA,
            pltpu.SemaphoreType.DMA,
            pltpu.SemaphoreType.DMA((FAR,)),
            pltpu.SemaphoreType.DMA((4,)),
            pltpu.SemaphoreType.DMA((4,)),
        ],
        cost_estimate=pl.CostEstimate(
            flops=2 * 10**9, bytes_accessed=10**6, transcendentals=0
        ),
        compiler_params=pltpu.CompilerParams(
            collective_id=0, has_side_effects=True, vmem_limit_bytes=VMEM_BYTES
        ),
    )(
        *(
            pltpu.with_memory_space_constraint(v, pltpu.HBM)
            for v in (
                adjoint.reshape(320, 128),
                flow.reshape(384, 128),
                point_cell.reshape(1, points),
                point_dest.reshape(1, points),
                point_target.reshape(1, points),
                point_weight.reshape(1, points),
            )
        ),
        point_count,
    )
    return out.reshape(1, 5, 8, 8, 128)


def solution(mesh):
    placed = (
        P("sec", None, "gx", "gy", None),
        P("sec", None, "gx", "gy", None),
        P("sec", "gx", "gy", None),
        P("sec", "gx", "gy", None),
        P("sec", "gx", "gy", None),
        P("sec", "gx", "gy", None),
        P("sec", "gx", "gy"),
    )
    return jax.shard_map(
        local,
        mesh=mesh,
        in_specs=placed,
        out_specs=P("sec", None, "gx", "gy", None),
        check_vma=False,
    )
```
